1024 devices in a mesh: lat: 16 (over x_hi, y), lon: 8 (over z), fsdp: 8 (over x_lo, core).
Axes of the slice: x: 8 (x_hi: 2, x_lo: 4; x = x_hi * 4 + x_lo), y: 8, z: 8, core: 2. Of those that a mesh axis runs over, the one named last changes fastest.
Arguments:
- latent: bfloat16 [8, 2, 96, 96, 512], P('fsdp', None, 'lat', 'lon'), may hold values from -6 to 6
- norm_gain: float32 [2, 512], replicated, may hold values from 0.1 to 1.9
- qkv_weight: bfloat16 [2, 512, 1536], P(None, 'fsdp'), may hold values from -0.25 to 0.25
- out_weight: bfloat16 [2, 512, 512], P(None, 'fsdp'), may hold values from -0.25 to 0.25
- rel_bias: float32 [2, 759, 16], replicated, may hold values from -4 to 304, as said below
- bias_index: int32 [144, 144], replicated, may hold values from 0 to 758
- region_ids: int32 [2, 96, 96], P(None, 'lat', 'lon'), may hold values from 0 to 3
Outputs:
- mixed: bfloat16 [8, 2, 96, 96, 512], P('fsdp', None, 'lat', 'lon')
The draws below stay inside these ranges and needn't reach their ends.
Inputs may be any that keep to these rules, and one draw needn't show every extreme that they name: `rel_bias`: in the hidden draw.
All inputs are finite; a program needn't handle non-finite values.
Results may differ from the reference program's by a relative error of at most 0.012.
Values may be sent and summed in bfloat16 or wider, within the bound.
A program may use at most 64 MiB of HBM per device.

```python
import jax
import jax.numpy as jnp
from jax import lax

D = 512
HEADS = 16
HEAD_DIM = 32
WZ = 2
WH = 6
WW = 12
WIN = 144
BIAS_ROWS = 759
LEVELS = 2
SAMPLES = 8
NLAT = 96
NLON = 96


def draw_rel_bias(key, part):
    values = jnp.clip(jax.random.normal(jax.random.fold_in(key, 11), (2, BIAS_ROWS, HEADS), jnp.float32), -4.0, 4.0)
    return values


def touch_ends(array, rng, smallest, largest):
    longest = array.shape.index(max(array.shape))
    spots = []
    for shift in (0, 1):
        where = [jax.random.randint(jax.random.fold_in(rng, axis), (), 0, length) for axis, length in enumerate(array.shape)]
        where[longest] = (where[longest] + shift) % array.shape[longest]
        spots.append(tuple(where))
    return array.at[spots[0]].set(smallest).at[spots[1]].set(largest)


def shard_levels(own_key, extent, cuts, low, top_value):
    def one(position, shards_of):
        draws = jax.random.uniform(jax.random.fold_in(jax.random.fold_in(own_key, 6), position), (shards_of,), jnp.float32, low / len(cuts), top_value / len(cuts))
        return jnp.repeat(jnp.exp(draws), extent[position] // shards_of).reshape((-1,) + (1,) * (len(extent) - position - 1))

    level = one(*cuts[0])
    for cut in cuts[1:]:
        level = level * one(*cut)
    return level


def gaussian(own_key, dims, scale, limit, shards=(), held_as=jnp.bfloat16):
    entries = jax.random.normal(own_key, dims, jnp.float32) * scale
    if len(shards) > 0:
        entries = shard_levels(own_key, dims, shards, -0.22, 0.18) * entries
    return jnp.clip(entries, min=-limit, max=limit).astype(held_as)


def setup_inputs(seed: int = 0) -> dict:
    key_of = jax.random.split(jax.random.key(seed), 8)
    latent = gaussian(key_of[0], (SAMPLES, LEVELS, NLAT, NLON, D), 1.0, 6.0, ((0, 8), (2, 16), (3, 8)))
    norm_gain = jnp.clip(1.0 + 0.18 * jax.random.normal(key_of[1], (2, D), jnp.float32), 0.1, 1.9)
    qkv_weight = gaussian(key_of[2], (2, D, 3 * D), D ** -0.5, 0.25, ((1, 8),))
    out_weight = gaussian(key_of[3], (2, D, D), D ** -0.5, 0.25, ((1, 8),))
    rel_bias = draw_rel_bias(jax.random.fold_in(key_of[7], 71), 0)
    bias_index = touch_ends(jax.random.randint(key_of[5], (WIN, WIN), 0, BIAS_ROWS), jax.random.fold_in(key_of[5], 1), 0, BIAS_ROWS - 1).astype(jnp.int32)
    region_ids = touch_ends(jax.random.randint(key_of[6], (LEVELS, NLAT, NLON), 0, 4), jax.random.fold_in(key_of[6], 1), 0, 3).astype(jnp.int32)
    return dict(latent=latent, norm_gain=norm_gain, qkv_weight=qkv_weight, out_weight=out_weight, rel_bias=rel_bias, bias_index=bias_index, region_ids=region_ids)


def layer_norm(hidden, gain_row):
    values = hidden.astype(jnp.float32)
    centre = lax.optimization_barrier(jnp.mean(values, axis=-1, keepdims=True))
    shifted = values - centre
    variance = lax.optimization_barrier(jnp.mean(shifted * shifted, axis=-1, keepdims=True))
    return (shifted * lax.rsqrt(variance + 1e-05) * gain_row).astype(jnp.bfloat16)

def bias_table(rel_bias, bias_index, block_index):
    return jnp.take(jnp.transpose(rel_bias[block_index]), bias_index, axis=1)

def split_bands(field_tile):
    level_count, row_count, col_count, feature_width = field_tile.shape
    pieces = field_tile.reshape(level_count // WZ, WZ, row_count // WH, WH, col_count // WW, WW, feature_width)
    pieces = jnp.transpose(pieces, (2, 0, 4, 1, 3, 5, 6))
    return pieces.reshape(row_count // WH, level_count // WZ * (col_count // WW), WIN, feature_width)

def merge_bands(band_windows, level_count, col_count):
    band_count = band_windows.shape[0]
    feature_width = band_windows.shape[3]
    pieces = band_windows.reshape(band_count, level_count // WZ, col_count // WW, WZ, WH, WW, feature_width)
    pieces = jnp.transpose(pieces, (1, 3, 0, 4, 2, 5, 6))
    return pieces.reshape(level_count, band_count * WH, col_count, feature_width)

def window_attention(normed, weight, bias_heads, region_tags):
    group_count = normed.shape[0]
    packed = jnp.dot(normed.reshape(-1, D), weight, preferred_element_type=jnp.float32).astype(jnp.bfloat16)
    packed = packed.reshape(group_count, WIN, 3, HEADS, HEAD_DIM)
    scores = jnp.einsum('gqhd,gkhd->ghqk', packed[:, :, 0].astype(jnp.float32), packed[:, :, 1].astype(jnp.float32))
    scores = scores * HEAD_DIM ** (-0.5) + bias_heads[None]
    if region_tags is not None:
        allowed = region_tags[:, :, None] == region_tags[:, None, :]
        scores = jnp.where(allowed[:, None], scores, -jnp.inf)
    row_peak = lax.optimization_barrier(jnp.max(scores, axis=-1, keepdims=True))
    exponent = jnp.exp(scores - row_peak)
    row_total = lax.optimization_barrier(jnp.sum(exponent, axis=-1, keepdims=True))
    attn_probs = (exponent / row_total).astype(jnp.bfloat16)
    mixed_out = jnp.einsum('ghqk,gkhd->gqhd', attn_probs.astype(jnp.float32), packed[:, :, 2].astype(jnp.float32))
    return mixed_out.astype(jnp.bfloat16).reshape(group_count, WIN, D)

def reference(latent, norm_gain, qkv_weight, out_weight, rel_bias, bias_index, region_ids):
    first_bias = bias_table(rel_bias, bias_index, 0)
    second_bias = bias_table(rel_bias, bias_index, 1)
    level_pos = lax.broadcasted_iota(jnp.int32, region_ids.shape, 0)
    row_pos = lax.broadcasted_iota(jnp.int32, region_ids.shape, 1)
    region_tags = region_ids * 4 + (level_pos == LEVELS - 1).astype(jnp.int32) * 2
    region_tags = region_tags + (row_pos >= NLAT - WH // 2).astype(jnp.int32)
    tag_bands = split_bands(region_tags[..., None])[..., 0]

    def first_band(band_rows):
        return window_attention(band_rows, qkv_weight[0], first_bias, None)

    def second_band(band_pair):
        return window_attention(band_pair[0], qkv_weight[1], second_bias, band_pair[1])

    def one_sample(sample):
        normed = layer_norm(sample, norm_gain[0])
        mixed_out = merge_bands(lax.map(first_band, split_bands(normed)), LEVELS, NLON)
        projected = jnp.dot(mixed_out.reshape(-1, D), out_weight[0], preferred_element_type=jnp.float32)
        middle = (sample.astype(jnp.float32) + projected.reshape(sample.shape)).astype(jnp.bfloat16)
        normed = layer_norm(middle, norm_gain[1])
        rolled = jnp.roll(normed, (-1, -(WH // 2), -(WW // 2)), axis=(0, 1, 2))
        mixed_out = lax.map(second_band, (split_bands(rolled), tag_bands))
        mixed_out = merge_bands(mixed_out, LEVELS, NLON)
        mixed_out = jnp.roll(mixed_out, (1, WH // 2, WW // 2), axis=(0, 1, 2))
        projected = jnp.dot(mixed_out.reshape(-1, D), out_weight[1], preferred_element_type=jnp.float32)
        return (middle.astype(jnp.float32) + projected.reshape(sample.shape)).astype(jnp.bfloat16)
    return lax.map(one_sample, latent)
```

```python
import functools

import jax
import jax.numpy as jnp
import numpy as np
from jax import lax
from jax.experimental import pallas as pl
from jax.experimental.pallas import tpu as pltpu
from jax.sharding import PartitionSpec as P

D = 512
HEADS = 16
HEAD_DIM = 32
WZ = 2
WH = 6
WW = 12
WIN = 144
HH = WH // 2
HW = WW // 2
QUAD = WZ * HH * HW
QPAD = 48
SPAD = 80
ROWS = WIN + 6 * SPAD
BIAS_ROWS = 759
LOG2E = 1.4426950408889634
SCALE = LOG2E * HEAD_DIM ** (-0.5)
BLOCKED = -1e30
MESH = pl.DeviceIdType.MESH
F32 = jnp.float32
BF16 = jnp.bfloat16


def token(z, h, w):
    return (z * WH + h) * WW + w


def one_hot_rows(sources, row_count, width):
    table = np.zeros((row_count, width), np.float32)
    for row, source in enumerate(sources):
        if source >= 0:
            table[row, source] = 1.0
    return table.astype(jnp.bfloat16)


@functools.cache
def selections():
    tokens = [(z, h, w) for z in range(WZ) for h in range(WH) for w in range(WW)]
    pad = [-1] * (SPAD - WIN // 2)
    north = [token(*t) for t in tokens if t[1] < HH] + pad
    south = [token(*t) for t in tokens if t[1] >= HH] + pad
    west = [token(*t) for t in tokens if t[2] < HW] + pad
    east = [token(*t) for t in tokens if t[2] >= HW] + pad
    strips = one_hot_rows(north + south + west + east, 4 * SPAD, WIN)

    def corner(first):
        rows = []
        for side in range(2):
            for z in range(WZ):
                for h in range(HH):
                    for w in range(HW):
                        rows.append(side * SPAD + (z * HH + h) * WW + first + w)
        return rows + pad

    corners = one_hot_rows(corner(0) + corner(HW), 2 * SPAD, 2 * SPAD)

    def source(z, row, col):
        n, s, w_, e, cw, ce = (WIN + k * SPAD for k in range(6))
        if HH <= row < HH + WH:
            h = row - HH
            if col < HW:
                return w_ + (z * WH + h) * HW + col
            if col < HW + WW:
                return token(z, h, col - HW)
            return e + (z * WH + h) * HW + col - HW - WW
        side = 0 if row < HH else 1
        h = row if row < HH else row - HH - WH
        if col < HW:
            return cw + side * QUAD + (z * HH + h) * HW + col
        if col < HW + WW:
            return (n, s)[side] + (z * HH + h) * WW + col - HW
        return ce + side * QUAD + (z * HH + h) * HW + col - HW - WW

    keys = []
    query_token = []
    query_place = []
    for a in range(2):
        for b in range(2):
            for dz, dh, dw in tokens:
                keys.append(source((dz + 1) % WZ, a * WH + dh, b * WW + dw))
            for z in range(WZ):
                for h in range(a * HH, a * HH + HH):
                    for w in range(b * HW, b * HW + HW):
                        query_token.append(token(z, h, w))
                        query_place.append(token((z - 1) % WZ, (h - HH) % WH, (w - HW) % WW))
            query_token += [-1] * (QPAD - QUAD)
            query_place += [-1] * (QPAD - QUAD)
    key_rows = one_hot_rows(keys, 4 * WIN, ROWS)
    query_rows = one_hot_rows(query_token, 4 * QPAD, WIN)
    place_rows = one_hot_rows(query_place, 4 * QPAD, 256)
    places = np.full((8, 256), -1, np.int32)
    for j, (dz, dh, dw) in enumerate(tokens):
        places[0, j] = dh * WZ + dz
        places[1, j] = dw
        places[2, j] = dz
        places[3, j] = dh
    return strips, corners, key_rows, query_rows, np.ascontiguousarray(query_rows.T), place_rows, places


def normalize(values, gain_row):
    centre = jnp.mean(values, axis=-1, keepdims=True)
    shifted = values - centre
    variance = jnp.mean(shifted * shifted, axis=-1, keepdims=True)
    return (shifted * lax.rsqrt(variance + 1e-05) * gain_row).astype(BF16)


def picked(table, places):
    return jnp.take_along_axis(table, places, axis=1, mode="promise_in_bounds")


def kernel(
    x_ref, gain_ref, qkv_ref, outw_ref, table_ref, idx_ref, region_ref,
    strip_ref, corner_ref, key_ref, query_ref, back_ref, place_ref, pos_ref,
    out_ref,
    wq, wo, table, index, index_out, regions, tags, allowed,
    bias0, bias1, normed, qkv0, mixed0, middle, rows, strip_out, corner_out, xq, xk, q1, kv1, mixed1,
    local_sem, send_sem, recv_sem,
    *, lat_count, lon_count,
):
    la, lo, fs = lax.axis_index("lat"), lax.axis_index("lon"), lax.axis_index("fsdp")
    y_count = lat_count // 2
    y, core, x = la % y_count, fs % 2, (la // y_count) * 4 + fs // 2

    def along_x(step):
        there = (x + step) % 8
        return ((there // 4) * y_count + y, lo, (there % 4) * 2 + core)

    right, left = along_x(1), along_x(7)
    sibling = (la, lo, fs + 1 - 2 * core)
    north = ((la + lat_count - 1) % lat_count, lo, fs)
    south = ((la + 1) % lat_count, lo, fs)
    west = (la, (lo + lon_count - 1) % lon_count, fs)
    east = (la, (lo + 1) % lon_count, fs)
    partners = (right, left, sibling, north, south, west, east)
    barrier = pltpu.get_barrier_semaphore()
    for partner in partners:
        pl.semaphore_signal(barrier, inc=1, device_id=partner, device_id_type=MESH)

    counter = [0]
    sent = []

    def send(source, target, device):
        copy = pltpu.make_async_remote_copy(
            src_ref=source, dst_ref=target, send_sem=send_sem.at[counter[0]], recv_sem=recv_sem.at[counter[0]],
            device_id=device, device_id_type=MESH,
        )
        counter[0] += 1
        copy.start()
        sent.append(copy)
        return copy

    shard = D // 8
    half = shard // 2
    weights = {0: (wq.at[0], qkv_ref.at[0]), 1: (wo.at[0], outw_ref.at[0]), 2: (wq.at[1], qkv_ref.at[1]), 3: (wo.at[1], outw_ref.at[1])}
    own_row = fs * shard
    from_right = right[2] * shard
    from_left = left[2] * shard
    across = ((fs + 4) % 8) * shard

    def part(ref, start, size):
        return ref.at[pl.ds(pl.multiple_of(start, half), size)]

    held = []
    for k in range(4):
        full, mine = weights[k]
        copy = pltpu.make_async_copy(mine, part(full, own_row, shard), local_sem.at[k])
        copy.start()
        held.append(copy)

    table[...] = jnp.zeros_like(table)
    table[:, :, :BIAS_ROWS] = table_ref[...] * LOG2E
    index[...] = jnp.zeros_like(index)
    index[:, :WIN] = idx_ref[...]
    pl.semaphore_wait(barrier, len(partners))

    stages = {}

    def start_weights(k):
        full, mine = weights[k]
        to_left = send(mine.at[pl.ds(0, half)], part(full, own_row, half), left)
        to_right = send(mine.at[pl.ds(half, half)], part(full, own_row + half, half), right)
        to_left2 = send(mine.at[pl.ds(half, half)], part(full, own_row + half, half), left)
        to_right2 = send(mine.at[pl.ds(0, half)], part(full, own_row, half), right)
        to_sibling = send(mine, part(full, own_row, shard), sibling)
        stages[k] = [to_left, to_right, to_left2, to_right2, to_sibling]

    def pass_first(k):
        full, _ = weights[k]
        first, second = stages[k][0], stages[k][1]
        first.wait_recv()
        low = part(full, from_right, half)
        relay_left = send(low, low, left)
        share_low = send(low, low, sibling)
        second.wait_recv()
        high = part(full, from_left + half, half)
        relay_right = send(high, high, right)
        share_high = send(high, high, sibling)
        stages[k] += [relay_left, relay_right, share_low, share_high]

    def pass_second(k):
        full, _ = weights[k]
        stages[k][2].wait_recv()
        high = part(full, from_right + half, half)
        share_high = send(high, high, sibling)
        stages[k][3].wait_recv()
        low = part(full, from_left, half)
        share_low = send(low, low, sibling)
        stages[k] += [share_high, share_low]

    def pass_across(k):
        full, _ = weights[k]
        stages[k][5].wait_recv()
        low = part(full, across, half)
        share_low = send(low, low, sibling)
        stages[k][6].wait_recv()
        high = part(full, across + half, half)
        share_high = send(high, high, sibling)
        stages[k] += [share_low, share_high]

    def finish_weights(k):
        held[k].wait()
        for at in (4, 7, 8, 9, 10, 11, 12):
            stages[k][at].wait_recv()

    start_weights(0)

    region_rows = jnp.zeros((16, 128), F32)
    regions[...] = region_rows
    for h in range(WH):
        regions[WZ * h : WZ * h + WZ, :WW] = region_ref[h].astype(F32)
    pos = pos_ref[...]
    row_hot = (lax.broadcasted_iota(jnp.int32, (16, 256), 0) == pos[0:1]).astype(F32)
    spread = lax.dot_general(regions[...], row_hot, (((0,), (0,)), ((), ())), preferred_element_type=F32)
    col_hot = lax.broadcasted_iota(jnp.int32, (128, 256), 0) == pos[1:2]
    region_row = jnp.sum(jnp.where(col_hot, spread, 0.0), axis=0, keepdims=True)
    last_rows = jnp.where(la == lat_count - 1, 1.0, 0.0) * (pos[3:4] >= HH).astype(F32)
    tag_row = region_row * 4.0 + 2.0 * (pos[2:3] == WZ - 1).astype(F32) + last_rows
    tags[3] = jnp.broadcast_to(tag_row, (8, 256))
    tag_south = send(tags.at[3], tags.at[1], south)
    tag_east = send(tags.at[3], tags.at[2], east)

    normed[...] = normalize(x_ref[...].astype(F32), gain_ref[0:1])

    def bias_rows0(first, count):
        @pl.loop(first, first + count)
        def _(r):
            span = pl.ds(pl.multiple_of(r * 8, 8), 8)
            for side in range(2):
                lanes = slice(side * 128, side * 128 + 128)
                places = index[span, lanes]
                lane = places & 127
                chunk = places >> 7
                for h in range(HEADS):
                    total = None
                    for c in range(6):
                        piece = picked(jnp.broadcast_to(table[0, h : h + 1, c * 128 : c * 128 + 128], (8, 128)), lane)
                        total = piece if total is None else jnp.where(chunk == c, piece, total)
                    bias0[h, span, lanes] = total

    def bias_rows1(first, count):
        @pl.loop(first, first + count)
        def _(r):
            span = pl.ds(pl.multiple_of(r * 8, 8), 8)
            window = r // 6
            inner = pl.ds(pl.multiple_of((r % 6) * 8, 8), 8)
            for side in range(2):
                lanes = slice(side * 128, side * 128 + 128)
                places = index_out[span, lanes]
                lane = places & 127
                chunk = places >> 7
                keep = allowed[span, lanes] > 0.5
                for h in range(HEADS):
                    total = None
                    for c in range(6):
                        piece = picked(jnp.broadcast_to(table[1, h : h + 1, c * 128 : c * 128 + 128], (8, 128)), lane)
                        total = piece if total is None else jnp.where(chunk == c, piece, total)
                    bias1[window, h, inner, lanes] = jnp.where(keep, total, BLOCKED)

    bias_rows0(0, 6)
    pass_first(0)
    tag_south.wait_recv()
    tag_corner = send(tags.at[1], tags.at[0], east)
    bias_rows0(6, 6)
    pass_second(0)
    start_weights(1)
    bias_rows0(12, 6)
    pass_across(0)
    finish_weights(0)

    @pl.loop(0, 6)
    def _(t):
        lanes = pl.ds(pl.multiple_of(t * 256, 256), 256)
        qkv0[:, lanes] = jnp.dot(normed[...], wq[0, :, lanes], preferred_element_type=F32).astype(BF16)

    pass_first(1)
    start_weights(2)
    lane_head = lax.broadcasted_iota(jnp.int32, (1, 128), 1) // HEAD_DIM

    @pl.loop(0, 4)
    def _(g):
        def cut(base):
            return qkv0[:, pl.ds(pl.multiple_of(base + g * 128, 128), 128)]

        q, k, v = cut(0), cut(D), cut(2 * D)
        v_ones = jnp.concatenate([v, jnp.ones((WIN, 128), BF16)], axis=1)
        top = jnp.zeros((WIN, 128), F32)
        bottom = jnp.zeros((WIN, 128), F32)
        for u in range(4):
            mine = lane_head == u
            scores = lax.dot_general(jnp.where(mine, q, jnp.zeros_like(q)), k, (((1,), (1,)), ((), ())), preferred_element_type=F32)
            scores = scores * SCALE + bias0[g * 4 + u, :, :WIN]
            peak = jnp.max(scores, axis=1, keepdims=True)
            weight = jnp.exp2(scores - peak).astype(BF16)
            both = jnp.dot(weight, v_ones, preferred_element_type=F32)
            top = jnp.where(mine, both[:, :128], top)
            bottom = jnp.where(mine, both[:, 128:], bottom)
        mixed0[:, pl.ds(pl.multiple_of(g * 128, 128), 128)] = (top / bottom).astype(BF16)

    pass_second(1)
    pass_across(1)
    finish_weights(1)
    projected = jnp.dot(mixed0[...], wo[0], preferred_element_type=F32)
    mid = (x_ref[...].astype(F32) + projected).astype(BF16)
    middle[...] = mid
    rows[0:WIN] = normalize(mid.astype(F32), gain_ref[1:2])
    strip_out[...] = jnp.dot(strip_ref[...], rows[0:WIN], preferred_element_type=F32).astype(BF16)

    def slot(k):
        return rows.at[pl.ds(WIN + k * SPAD, SPAD)]

    to_north = send(strip_out.at[pl.ds(0, SPAD)], slot(1), north)
    to_south = send(strip_out.at[pl.ds(SPAD, SPAD)], slot(0), south)
    to_west = send(strip_out.at[pl.ds(2 * SPAD, SPAD)], slot(3), west)
    to_east = send(strip_out.at[pl.ds(3 * SPAD, SPAD)], slot(2), east)

    pass_first(2)
    xq[...] = jnp.dot(query_ref[...], rows[0:WIN], preferred_element_type=F32).astype(BF16)
    places = index[...]
    index_lane = jnp.dot(place_ref[:, :WIN], (places & 127).astype(F32).astype(BF16), preferred_element_type=F32)
    index_chunk = jnp.dot(place_ref[:, :WIN], (places >> 7).astype(F32).astype(BF16), preferred_element_type=F32)
    index_out[...] = (index_chunk * 128.0 + index_lane).astype(jnp.int32)
    tag_east.wait_recv()
    tag_corner.wait_recv()
    for w in range(4):
        span = slice(w * QPAD, w * QPAD + QPAD)
        query_tags = lax.dot_general(place_ref[span], tags[w].astype(BF16), (((1,), (1,)), ((), ())), preferred_element_type=F32)
        allowed[span] = jnp.where(query_tags[:, 0:1] == tags[w, 0:1], 1.0, 0.0)
    bias_rows1(0, 8)
    pass_second(2)
    start_weights(3)
    bias_rows1(8, 8)
    pass_across(2)
    pass_first(3)
    to_north.wait_recv()
    to_south.wait_recv()
    corner_out[...] = jnp.dot(corner_ref[...], rows[WIN : WIN + 2 * SPAD], preferred_element_type=F32).astype(BF16)
    corner_west = send(corner_out.at[pl.ds(0, SPAD)], slot(5), west)
    corner_east = send(corner_out.at[pl.ds(SPAD, SPAD)], slot(4), east)
    bias_rows1(16, 8)
    pass_second(3)
    finish_weights(2)

    @pl.loop(0, 2)
    def _(t):
        lanes = pl.ds(pl.multiple_of(t * 256, 256), 256)
        q1[:, lanes] = jnp.dot(xq[...], wq[1, :, lanes], preferred_element_type=F32).astype(BF16)

    pass_across(3)
    to_west.wait_recv()
    to_east.wait_recv()
    corner_west.wait_recv()
    corner_east.wait_recv()

    @pl.loop(0, 4)
    def _(t):
        span = pl.ds(pl.multiple_of(t * WIN, 16), WIN)
        xk[span] = jnp.dot(key_ref[span], rows[...], preferred_element_type=F32).astype(BF16)

    @pl.loop(0, 4)
    def _(t):
        lanes = pl.ds(pl.multiple_of(t * 256, 256), 256)
        source = pl.ds(pl.multiple_of(D + t * 256, 256), 256)
        kv1[:, lanes] = jnp.dot(xk[...], wq[1, :, source], preferred_element_type=F32).astype(BF16)

    @pl.loop(0, 4)
    def _(g):
        for w in range(4):
            span = slice(w * QPAD, w * QPAD + QPAD)
            keys = slice(w * WIN, w * WIN + WIN)
            q = q1[span, pl.ds(pl.multiple_of(g * 128, 128), 128)]
            k = kv1[keys, pl.ds(pl.multiple_of(g * 128, 128), 128)]
            v = kv1[keys, pl.ds(pl.multiple_of(D + g * 128, 128), 128)]
            v_ones = jnp.concatenate([v, jnp.ones((WIN, 128), BF16)], axis=1)
            stacked = jnp.concatenate([jnp.where(lane_head == u, q, jnp.zeros_like(q)) for u in range(4)], axis=0)
            scores = lax.dot_general(stacked, k, (((1,), (1,)), ((), ())), preferred_element_type=F32)
            bias = bias1[w, pl.ds(g * 4, 4), :, :WIN].reshape(4 * QPAD, WIN)
            scores = scores * SCALE + bias
            peak = jnp.max(scores, axis=1, keepdims=True)
            weight = jnp.exp2(scores - peak).astype(BF16)
            both = jnp.dot(weight, v_ones, preferred_element_type=F32)
            top, bottom = both[:QPAD, :128], both[:QPAD, 128:]
            for u in range(1, 4):
                mine = lane_head == u
                top = jnp.where(mine, both[u * QPAD : u * QPAD + QPAD, :128], top)
                bottom = jnp.where(mine, both[u * QPAD : u * QPAD + QPAD, 128:], bottom)
            mixed1[span, pl.ds(pl.multiple_of(g * 128, 128), 128)] = (top / bottom).astype(BF16)

    finish_weights(3)
    natural = jnp.dot(back_ref[...], mixed1[...], preferred_element_type=F32).astype(BF16)
    projected = jnp.dot(natural, wo[1], preferred_element_type=F32)
    out_ref[...] = (middle[...].astype(F32) + projected).astype(BF16)
    for copy in sent:
        copy.wait_send()


COPIES = 4 * 13 + 3 + 6


def local(lat_count, lon_count, latent, norm_gain, qkv_weight, out_weight, rel_bias, bias_index, region_ids):
    vmem = pl.BlockSpec(memory_space=pltpu.VMEM)
    anywhere = pl.BlockSpec(memory_space=pl.ANY)
    out = pl.pallas_call(
        functools.partial(kernel, lat_count=lat_count, lon_count=lon_count),
        out_shape=jax.ShapeDtypeStruct((WIN, D), BF16),
        in_specs=[vmem, vmem, anywhere, anywhere] + [vmem] * 10,
        out_specs=vmem,
        scratch_shapes=[
            pltpu.VMEM((2, D, 3 * D), BF16),
            pltpu.VMEM((2, D, D), BF16),
            pltpu.VMEM((2, HEADS, 768), F32),
            pltpu.VMEM((WIN, 256), jnp.int32),
            pltpu.VMEM((4 * QPAD, 256), jnp.int32),
            pltpu.VMEM((16, 128), F32),
            pltpu.VMEM((4, 8, 256), F32),
            pltpu.VMEM((4 * QPAD, 256), F32),
            pltpu.VMEM((HEADS, WIN, 256), F32),
            pltpu.VMEM((4, HEADS, QPAD, 256), F32),
            pltpu.VMEM((WIN, D), BF16),
            pltpu.VMEM((WIN, 3 * D), BF16),
            pltpu.VMEM((WIN, D), BF16),
            pltpu.VMEM((WIN, D), BF16),
            pltpu.VMEM((ROWS, D), BF16),
            pltpu.VMEM((4 * SPAD, D), BF16),
            pltpu.VMEM((2 * SPAD, D), BF16),
            pltpu.VMEM((4 * QPAD, D), BF16),
            pltpu.VMEM((4 * WIN, D), BF16),
            pltpu.VMEM((4 * QPAD, D), BF16),
            pltpu.VMEM((4 * WIN, 2 * D), BF16),
            pltpu.VMEM((4 * QPAD, D), BF16),
            pltpu.SemaphoreType.DMA((4,)),
            pltpu.SemaphoreType.DMA((COPIES,)),
            pltpu.SemaphoreType.DMA((COPIES,)),
        ],
        compiler_params=pltpu.CompilerParams(
            collective_id=0, has_side_effects=True, vmem_limit_bytes=48 * 2**20
        ),
        name="two_blocks",
    )(
        latent.reshape(WIN, D), norm_gain, qkv_weight, out_weight,
        jnp.transpose(rel_bias, (0, 2, 1)), bias_index, jnp.transpose(region_ids, (1, 0, 2)),
        *(jnp.asarray(s) for s in selections()),
    )
    return out.reshape(latent.shape)


def solution(mesh):
    return jax.shard_map(
        functools.partial(local, mesh.shape["lat"], mesh.shape["lon"]),
        mesh=mesh,
        in_specs=(
            P("fsdp", None, "lat", "lon", None),
            P(),
            P(None, "fsdp", None),
            P(None, "fsdp", None),
            P(),
            P(),
            P(None, "lat", "lon"),
        ),
        out_specs=P("fsdp", None, "lat", "lon", None),
        check_vma=False,
    )
```

```python
import functools

import jax
import jax.numpy as jnp
import numpy as np
from jax import lax
from jax.experimental import pallas as pl
from jax.experimental.pallas import tpu as pltpu
from jax.sharding import PartitionSpec as P

D = 512
HEADS = 16
HEAD_DIM = 32
WZ = 2
WH = 6
WW = 12
WIN = 144
HH = WH // 2
HW = WW // 2
QUAD = WZ * HH * HW
QPAD = 48
SPAD = 80
ROWS = WIN + 6 * SPAD
BIAS_ROWS = 759
LOG2E = 1.4426950408889634
SCALE = LOG2E * HEAD_DIM ** (-0.5)
BLOCKED = -1e30
MESH = pl.DeviceIdType.MESH
F32 = jnp.float32
BF16 = jnp.bfloat16


def token(z, h, w):
    return (z * WH + h) * WW + w


def one_hot_rows(sources, row_count, width):
    table = np.zeros((row_count, width), np.float32)
    for row, source in enumerate(sources):
        if source >= 0:
            table[row, source] = 1.0
    return table.astype(jnp.bfloat16)


@functools.cache
def selections():
    tokens = [(z, h, w) for z in range(WZ) for h in range(WH) for w in range(WW)]
    pad = [-1] * (SPAD - WIN // 2)
    north = [token(*t) for t in tokens if t[1] < HH] + pad
    south = [token(*t) for t in tokens if t[1] >= HH] + pad
    west = [token(*t) for t in tokens if t[2] < HW] + pad
    east = [token(*t) for t in tokens if t[2] >= HW] + pad
    strips = one_hot_rows(north + south + west + east, 4 * SPAD, WIN)

    def corner(first):
        rows = []
        for side in range(2):
            for z in range(WZ):
                for h in range(HH):
                    for w in range(HW):
                        rows.append(side * SPAD + (z * HH + h) * WW + first + w)
        return rows + pad

    corners = one_hot_rows(corner(0) + corner(HW), 2 * SPAD, 2 * SPAD)

    def source(z, row, col):
        n, s, w_, e, cw, ce = (WIN + k * SPAD for k in range(6))
        if HH <= row < HH + WH:
            h = row - HH
            if col < HW:
                return w_ + (z * WH + h) * HW + col
            if col < HW + WW:
                return token(z, h, col - HW)
            return e + (z * WH + h) * HW + col - HW - WW
        side = 0 if row < HH else 1
        h = row if row < HH else row - HH - WH
        if col < HW:
            return cw + side * QUAD + (z * HH + h) * HW + col
        if col < HW + WW:
            return (n, s)[side] + (z * HH + h) * WW + col - HW
        return ce + side * QUAD + (z * HH + h) * HW + col - HW - WW

    keys = []
    query_token = []
    query_place = []
    for a in range(2):
        for b in range(2):
            for dz, dh, dw in tokens:
                keys.append(source((dz + 1) % WZ, a * WH + dh, b * WW + dw))
            for z in range(WZ):
                for h in range(a * HH, a * HH + HH):
                    for w in range(b * HW, b * HW + HW):
                        query_token.append(token(z, h, w))
                        query_place.append(token((z - 1) % WZ, (h - HH) % WH, (w - HW) % WW))
            query_token += [-1] * (QPAD - QUAD)
            query_place += [-1] * (QPAD - QUAD)
    key_rows = one_hot_rows(keys, 4 * WIN, ROWS)
    query_rows = one_hot_rows(query_token, 4 * QPAD, WIN)
    place_rows = one_hot_rows(query_place, 4 * QPAD, 256)
    places = np.full((8, 256), -1, np.int32)
    for j, (dz, dh, dw) in enumerate(tokens):
        places[0, j] = dh * WZ + dz
        places[1, j] = dw
        places[2, j] = dz
        places[3, j] = dh
    return strips, corners, key_rows, query_rows, np.ascontiguousarray(query_rows.T), place_rows, places


def normalize(values, gain_row):
    centre = jnp.mean(values, axis=-1, keepdims=True)
    shifted = values - centre
    variance = jnp.mean(shifted * shifted, axis=-1, keepdims=True)
    return (shifted * lax.rsqrt(variance + 1e-05) * gain_row).astype(BF16)


def picked(table, places):
    return jnp.take_along_axis(table, places, axis=1, mode="promise_in_bounds")


def kernel(
    x_hbm, gain_hbm, qkv_ref, outw_ref, table_hbm, idx_hbm, region_hbm,
    strip_hbm, corner_hbm, key_hbm, query_hbm, back_hbm, place_hbm, pos_hbm,
    out_ref,
    x_ref, gain_ref, table_ref, idx_ref, region_ref,
    strip_ref, corner_ref, key_ref, query_ref, back_ref, place_ref, pos_ref,
    wq, wo, table, index, index_out, regions, tags, allowed,
    bias0, bias1, normed, qkv0, mixed0, middle, rows, strip_out, corner_out, xq, xk, q1, kv1, mixed1,
    load_sem, local_sem, send_sem, recv_sem,
    *, lat_count, lon_count,
):
    la, lo, fs = lax.axis_index("lat"), lax.axis_index("lon"), lax.axis_index("fsdp")
    y_count = lat_count // 2
    y, core, x = la % y_count, fs % 2, (la // y_count) * 4 + fs // 2

    def along_x(step):
        there = (x + step) % 8
        return ((there // 4) * y_count + y, lo, (there % 4) * 2 + core)

    right, left = along_x(1), along_x(7)
    sibling = (la, lo, fs + 1 - 2 * core)
    north = ((la + lat_count - 1) % lat_count, lo, fs)
    south = ((la + 1) % lat_count, lo, fs)
    west = (la, (lo + lon_count - 1) % lon_count, fs)
    east = (la, (lo + 1) % lon_count, fs)
    partners = (right, left, sibling, north, south, west, east)
    barrier = pltpu.get_barrier_semaphore()
    for partner in partners:
        pl.semaphore_signal(barrier, inc=1, device_id=partner, device_id_type=MESH)

    loads = []
    for k, (source, target) in enumerate((
        (table_hbm, table_ref), (idx_hbm, idx_ref), (x_hbm, x_ref), (gain_hbm, gain_ref), (region_hbm, region_ref),
        (pos_hbm, pos_ref), (place_hbm, place_ref), (query_hbm, query_ref), (strip_hbm, strip_ref),
        (corner_hbm, corner_ref), (key_hbm, key_ref), (back_hbm, back_ref),
    )):
        copy = pltpu.make_async_copy(source, target, load_sem.at[k])
        copy.start()
        loads.append(copy)

    counter = [0]
    sent = []

    def send(source, target, device):
        copy = pltpu.make_async_remote_copy(
            src_ref=source, dst_ref=target, send_sem=send_sem.at[counter[0]], recv_sem=recv_sem.at[counter[0]],
            device_id=device, device_id_type=MESH,
        )
        counter[0] += 1
        copy.start()
        sent.append(copy)
        return copy

    shard = D // 8
    half = shard // 2
    weights = {0: (wq.at[0], qkv_ref.at[0]), 1: (wo.at[0], outw_ref.at[0]), 2: (wq.at[1], qkv_ref.at[1]), 3: (wo.at[1], outw_ref.at[1])}
    own_row = fs * shard
    from_right = right[2] * shard
    from_left = left[2] * shard
    across = ((fs + 4) % 8) * shard

    def part(ref, start, size):
        return ref.at[pl.ds(pl.multiple_of(start, half), size)]

    held = []
    for k in range(4):
        full, mine = weights[k]
        copy = pltpu.make_async_copy(mine, part(full, own_row, shard), local_sem.at[k])
        copy.start()
        held.append(copy)

    pl.semaphore_wait(barrier, len(partners))

    stages = {}

    def start_weights(k):
        full, mine = weights[k]
        to_left = send(mine.at[pl.ds(0, half)], part(full, own_row, half), left)
        to_right = send(mine.at[pl.ds(half, half)], part(full, own_row + half, half), right)
        to_left2 = send(mine.at[pl.ds(half, half)], part(full, own_row + half, half), left)
        to_right2 = send(mine.at[pl.ds(0, half)], part(full, own_row, half), right)
        to_sibling = send(mine, part(full, own_row, shard), sibling)
        stages[k] = [to_left, to_right, to_left2, to_right2, to_sibling]

    def pass_first(k):
        full, _ = weights[k]
        first, second = stages[k][0], stages[k][1]
        first.wait_recv()
        low = part(full, from_right, half)
        relay_left = send(low, low, left)
        share_low = send(low, low, sibling)
        second.wait_recv()
        high = part(full, from_left + half, half)
        relay_right = send(high, high, right)
        share_high = send(high, high, sibling)
        stages[k] += [relay_left, relay_right, share_low, share_high]

    def pass_second(k):
        full, _ = weights[k]
        stages[k][2].wait_recv()
        high = part(full, from_right + half, half)
        share_high = send(high, high, sibling)
        stages[k][3].wait_recv()
        low = part(full, from_left, half)
        share_low = send(low, low, sibling)
        stages[k] += [share_high, share_low]

    def pass_across(k):
        full, _ = weights[k]
        stages[k][5].wait_recv()
        low = part(full, across, half)
        share_low = send(low, low, sibling)
        stages[k][6].wait_recv()
        high = part(full, across + half, half)
        share_high = send(high, high, sibling)
        stages[k] += [share_low, share_high]

    def finish_weights(k):
        held[k].wait()
        for at in (4, 7, 8, 9, 10, 11, 12):
            stages[k][at].wait_recv()

    start_weights(0)

    table[...] = jnp.zeros_like(table)
    index[...] = jnp.zeros_like(index)
    for copy in loads[:8]:
        copy.wait()
    table[:, :, :BIAS_ROWS] = table_ref[...] * LOG2E
    index[:, :WIN] = idx_ref[...]

    region_rows = jnp.zeros((16, 128), F32)
    regions[...] = region_rows
    for h in range(WH):
        regions[WZ * h : WZ * h + WZ, :WW] = region_ref[h].astype(F32)
    pos = pos_ref[...]
    row_hot = (lax.broadcasted_iota(jnp.int32, (16, 256), 0) == pos[0:1]).astype(F32)
    spread = lax.dot_general(regions[...], row_hot, (((0,), (0,)), ((), ())), preferred_element_type=F32)
    col_hot = lax.broadcasted_iota(jnp.int32, (128, 256), 0) == pos[1:2]
    region_row = jnp.sum(jnp.where(col_hot, spread, 0.0), axis=0, keepdims=True)
    last_rows = jnp.where(la == lat_count - 1, 1.0, 0.0) * (pos[3:4] >= HH).astype(F32)
    tag_row = region_row * 4.0 + 2.0 * (pos[2:3] == WZ - 1).astype(F32) + last_rows
    tags[3] = jnp.broadcast_to(tag_row, (8, 256))
    tag_south = send(tags.at[3], tags.at[1], south)
    tag_east = send(tags.at[3], tags.at[2], east)

    normed[...] = normalize(x_ref[...].astype(F32), gain_ref[0:1])

    places = index[...]
    index_lane = jnp.dot(place_ref[:, :WIN], (places & 127).astype(F32).astype(BF16), preferred_element_type=F32)
    index_chunk = jnp.dot(place_ref[:, :WIN], (places >> 7).astype(F32).astype(BF16), preferred_element_type=F32)
    index_out[...] = (index_chunk * 128.0 + index_lane).astype(jnp.int32)
    def gathered(block, places):
        lane = places & 127
        chunk = places >> 7
        masks = [chunk == c for c in range(1, 6)]
        for h in range(HEADS):
            total = None
            for c in range(6):
                piece = picked(jnp.broadcast_to(table[block, h : h + 1, c * 128 : c * 128 + 128], (8, 128)), lane)
                total = piece if total is None else jnp.where(masks[c - 1], piece, total)
            yield h, total

    def bias_rows0(first, count):
        @pl.loop(first, first + count)
        def _(r):
            span = pl.ds(pl.multiple_of(r * 8, 8), 8)
            for lanes in (slice(0, 128), slice(128, 256)):
                for h, total in gathered(0, index[span, lanes]):
                    bias0[h, span, lanes] = total

    def bias_rows1(first, count):
        @pl.loop(first, first + count)
        def _(r):
            span = pl.ds(pl.multiple_of(r * 8, 8), 8)
            window = r // 6
            inner = pl.ds(pl.multiple_of((r % 6) * 8, 8), 8)
            for lanes in (slice(0, 128), slice(128, 256)):
                keep = allowed[span, lanes] > 0.5
                for h, total in gathered(1, index_out[span, lanes]):
                    bias1[window, h, inner, lanes] = jnp.where(keep, total, BLOCKED)

    bias_rows0(0, 9)
    pass_first(0)
    tag_south.wait_recv()
    tag_corner = send(tags.at[1], tags.at[0], east)
    bias_rows0(9, 9)
    pass_second(0)
    start_weights(1)
    tag_east.wait_recv()
    tag_corner.wait_recv()
    for w in range(4):
        span = slice(w * QPAD, w * QPAD + QPAD)
        query_tags = lax.dot_general(place_ref[span], tags[w].astype(BF16), (((1,), (1,)), ((), ())), preferred_element_type=F32)
        allowed[span] = jnp.where(query_tags[:, 0:1] == tags[w, 0:1], 1.0, 0.0)
    bias_rows1(0, 12)
    pass_across(0)
    finish_weights(0)

    @pl.loop(0, 6)
    def _(t):
        lanes = pl.ds(pl.multiple_of(t * 256, 256), 256)
        qkv0[:, lanes] = jnp.dot(normed[...], wq[0, :, lanes], preferred_element_type=F32).astype(BF16)

    pass_first(1)
    start_weights(2)
    lane_head = lax.broadcasted_iota(jnp.int32, (1, 128), 1) // HEAD_DIM

    @pl.loop(0, 4)
    def _(g):
        def cut(base):
            return qkv0[:, pl.ds(pl.multiple_of(base + g * 128, 128), 128)]

        q, k, v = cut(0), cut(D), cut(2 * D)
        v_ones = jnp.concatenate([v, jnp.ones((WIN, 128), BF16)], axis=1)
        top = jnp.zeros((WIN, 128), F32)
        bottom = jnp.zeros((WIN, 128), F32)
        for u in range(4):
            mine = lane_head == u
            scores = lax.dot_general(jnp.where(mine, q, jnp.zeros_like(q)), k, (((1,), (1,)), ((), ())), preferred_element_type=F32)
            scores = scores * SCALE + bias0[g * 4 + u, :, :WIN]
            peak = jnp.max(scores, axis=1, keepdims=True)
            weight = jnp.exp2(scores - peak).astype(BF16)
            both = jnp.dot(weight, v_ones, preferred_element_type=F32)
            top = jnp.where(mine, both[:, :128], top)
            bottom = jnp.where(mine, both[:, 128:], bottom)
        mixed0[:, pl.ds(pl.multiple_of(g * 128, 128), 128)] = (top / bottom).astype(BF16)

    pass_second(1)
    pass_across(1)
    finish_weights(1)
    for copy in loads[8:]:
        copy.wait()
    projected = jnp.dot(mixed0[...], wo[0], preferred_element_type=F32)
    mid = (x_ref[...].astype(F32) + projected).astype(BF16)
    middle[...] = mid
    rows[0:WIN] = normalize(mid.astype(F32), gain_ref[1:2])
    strip_out[...] = jnp.dot(strip_ref[...], rows[0:WIN], preferred_element_type=F32).astype(BF16)

    def slot(k):
        return rows.at[pl.ds(WIN + k * SPAD, SPAD)]

    to_north = send(strip_out.at[pl.ds(0, SPAD)], slot(1), north)
    to_south = send(strip_out.at[pl.ds(SPAD, SPAD)], slot(0), south)
    to_west = send(strip_out.at[pl.ds(2 * SPAD, SPAD)], slot(3), west)
    to_east = send(strip_out.at[pl.ds(3 * SPAD, SPAD)], slot(2), east)

    pass_first(2)
    xq[...] = jnp.dot(query_ref[...], rows[0:WIN], preferred_element_type=F32).astype(BF16)
    bias_rows1(12, 6)
    pass_second(2)
    start_weights(3)
    bias_rows1(18, 6)
    pass_across(2)
    finish_weights(2)
    pass_first(3)
    @pl.loop(0, 2)
    def _(t):
        lanes = pl.ds(pl.multiple_of(t * 256, 256), 256)
        q1[:, lanes] = jnp.dot(xq[...], wq[1, :, lanes], preferred_element_type=F32).astype(BF16)

    to_north.wait_recv()
    to_south.wait_recv()
    corner_out[...] = jnp.dot(corner_ref[...], rows[WIN : WIN + 2 * SPAD], preferred_element_type=F32).astype(BF16)
    corner_west = send(corner_out.at[pl.ds(0, SPAD)], slot(5), west)
    corner_east = send(corner_out.at[pl.ds(SPAD, SPAD)], slot(4), east)
    pass_second(3)
    pass_across(3)
    to_west.wait_recv()
    to_east.wait_recv()
    corner_west.wait_recv()
    corner_east.wait_recv()

    @pl.loop(0, 4)
    def _(t):
        span = pl.ds(pl.multiple_of(t * WIN, 16), WIN)
        xk[span] = jnp.dot(key_ref[span], rows[...], preferred_element_type=F32).astype(BF16)

    @pl.loop(0, 4)
    def _(t):
        lanes = pl.ds(pl.multiple_of(t * 256, 256), 256)
        source = pl.ds(pl.multiple_of(D + t * 256, 256), 256)
        kv1[:, lanes] = jnp.dot(xk[...], wq[1, :, source], preferred_element_type=F32).astype(BF16)

    @pl.loop(0, 4)
    def _(g):
        for w in range(4):
            span = slice(w * QPAD, w * QPAD + QPAD)
            keys = slice(w * WIN, w * WIN + WIN)
            q = q1[span, pl.ds(pl.multiple_of(g * 128, 128), 128)]
            k = kv1[keys, pl.ds(pl.multiple_of(g * 128, 128), 128)]
            v = kv1[keys, pl.ds(pl.multiple_of(D + g * 128, 128), 128)]
            v_ones = jnp.concatenate([v, jnp.ones((WIN, 128), BF16)], axis=1)
            stacked = jnp.concatenate([jnp.where(lane_head == u, q, jnp.zeros_like(q)) for u in range(4)], axis=0)
            scores = lax.dot_general(stacked, k, (((1,), (1,)), ((), ())), preferred_element_type=F32)
            bias = bias1[w, pl.ds(g * 4, 4), :, :WIN].reshape(4 * QPAD, WIN)
            scores = scores * SCALE + bias
            peak = jnp.max(scores, axis=1, keepdims=True)
            weight = jnp.exp2(scores - peak).astype(BF16)
            both = jnp.dot(weight, v_ones, preferred_element_type=F32)
            top, bottom = both[:QPAD, :128], both[:QPAD, 128:]
            for u in range(1, 4):
                mine = lane_head == u
                top = jnp.where(mine, both[u * QPAD : u * QPAD + QPAD, :128], top)
                bottom = jnp.where(mine, both[u * QPAD : u * QPAD + QPAD, 128:], bottom)
            mixed1[span, pl.ds(pl.multiple_of(g * 128, 128), 128)] = (top / bottom).astype(BF16)

    finish_weights(3)
    natural = jnp.dot(back_ref[...], mixed1[...], preferred_element_type=F32).astype(BF16)
    projected = jnp.dot(natural, wo[1], preferred_element_type=F32)
    out_ref[...] = (middle[...].astype(F32) + projected).astype(BF16)
    for copy in sent:
        copy.wait_send()


COPIES = 4 * 13 + 3 + 6


def local(lat_count, lon_count, latent, norm_gain, qkv_weight, out_weight, rel_bias, bias_index, region_ids):
    operands = (
        latent.reshape(WIN, D), norm_gain, qkv_weight, out_weight,
        jnp.transpose(rel_bias, (0, 2, 1)), bias_index, jnp.transpose(region_ids, (1, 0, 2)),
        *(jnp.asarray(s) for s in selections()),
    )
    vmem = pl.BlockSpec(memory_space=pltpu.VMEM)
    out = pl.pallas_call(
        functools.partial(kernel, lat_count=lat_count, lon_count=lon_count),
        out_shape=jax.ShapeDtypeStruct((WIN, D), BF16),
        in_specs=[pl.BlockSpec(memory_space=pltpu.HBM)] * 14,
        out_specs=vmem,
        scratch_shapes=[pltpu.VMEM(a.shape, a.dtype) for k, a in enumerate(operands) if k not in (2, 3)] + [
            pltpu.VMEM((2, D, 3 * D), BF16),
            pltpu.VMEM((2, D, D), BF16),
            pltpu.VMEM((2, HEADS, 768), F32),
            pltpu.VMEM((WIN, 256), jnp.int32),
            pltpu.VMEM((4 * QPAD, 256), jnp.int32),
            pltpu.VMEM((16, 128), F32),
            pltpu.VMEM((4, 8, 256), F32),
            pltpu.VMEM((4 * QPAD, 256), F32),
            pltpu.VMEM((HEADS, WIN, 256), F32),
            pltpu.VMEM((4, HEADS, QPAD, 256), F32),
            pltpu.VMEM((WIN, D), BF16),
            pltpu.VMEM((WIN, 3 * D), BF16),
            pltpu.VMEM((WIN, D), BF16),
            pltpu.VMEM((WIN, D), BF16),
            pltpu.VMEM((ROWS, D), BF16),
            pltpu.VMEM((4 * SPAD, D), BF16),
            pltpu.VMEM((2 * SPAD, D), BF16),
            pltpu.VMEM((4 * QPAD, D), BF16),
            pltpu.VMEM((4 * WIN, D), BF16),
            pltpu.VMEM((4 * QPAD, D), BF16),
            pltpu.VMEM((4 * WIN, 2 * D), BF16),
            pltpu.VMEM((4 * QPAD, D), BF16),
            pltpu.SemaphoreType.DMA((12,)),
            pltpu.SemaphoreType.DMA((4,)),
            pltpu.SemaphoreType.DMA((COPIES,)),
            pltpu.SemaphoreType.DMA((COPIES,)),
        ],
        compiler_params=pltpu.CompilerParams(
            collective_id=0, has_side_effects=True, vmem_limit_bytes=60 * 2**20
        ),
        name="two_blocks",
    )(*operands)
    return out.reshape(latent.shape)


def solution(mesh):
    return jax.shard_map(
        functools.partial(local, mesh.shape["lat"], mesh.shape["lon"]),
        mesh=mesh,
        in_specs=(
            P("fsdp", None, "lat", "lon", None),
            P(),
            P(None, "fsdp", None),
            P(None, "fsdp", None),
            P(),
            P(),
            P(None, "lat", "lon"),
        ),
        out_specs=P("fsdp", None, "lat", "lon", None),
        check_vma=False,
    )
```

```python
import functools

import jax
import jax.numpy as jnp
import numpy as np
from jax import lax
from jax.experimental import pallas as pl
from jax.experimental.pallas import tpu as pltpu
from jax.sharding import PartitionSpec as P

D = 512
HEADS = 16
HEAD_DIM = 32
WZ = 2
WH = 6
WW = 12
WIN = 144
HH = WH // 2
HW = WW // 2
QUAD = WZ * HH * HW
QPAD = 40
SPAD = 80
EARLY = 512
ROWS = EARLY + 2 * SPAD
SLOTS = tuple(WIN + k * SPAD for k in range(4)) + (EARLY, EARLY + SPAD)
BIAS_ROWS = 759
LOG2E = 1.4426950408889634
SCALE = LOG2E * HEAD_DIM ** (-0.5)
BLOCKED = -1e30
MESH = pl.DeviceIdType.MESH
F32 = jnp.float32
BF16 = jnp.bfloat16


def token(z, h, w):
    return (z * WH + h) * WW + w


def one_hot_rows(sources, row_count, width):
    table = np.zeros((row_count, width), np.float32)
    for row, source in enumerate(sources):
        if source >= 0:
            table[row, source] = 1.0
    return table.astype(jnp.bfloat16)


@functools.cache
def selections():
    tokens = [(z, h, w) for z in range(WZ) for h in range(WH) for w in range(WW)]
    pad = [-1] * (SPAD - WIN // 2)
    north = [token(*t) for t in tokens if t[1] < HH] + pad
    south = [token(*t) for t in tokens if t[1] >= HH] + pad
    west = [token(*t) for t in tokens if t[2] < HW] + pad
    east = [token(*t) for t in tokens if t[2] >= HW] + pad
    strips = one_hot_rows(north + south + west + east, 4 * SPAD, WIN)

    def corner(first):
        rows = []
        for side in range(2):
            for z in range(WZ):
                for h in range(HH):
                    for w in range(HW):
                        rows.append(side * SPAD + (z * HH + h) * WW + first + w)
        return rows + pad

    corners = one_hot_rows(corner(0) + corner(HW), 2 * SPAD, 2 * SPAD)

    def source(z, row, col):
        n, s, w_, e, cw, ce = SLOTS
        if HH <= row < HH + WH:
            h = row - HH
            if col < HW:
                return w_ + (z * WH + h) * HW + col
            if col < HW + WW:
                return token(z, h, col - HW)
            return e + (z * WH + h) * HW + col - HW - WW
        side = 0 if row < HH else 1
        h = row if row < HH else row - HH - WH
        if col < HW:
            return cw + side * QUAD + (z * HH + h) * HW + col
        if col < HW + WW:
            return (n, s)[side] + (z * HH + h) * WW + col - HW
        return ce + side * QUAD + (z * HH + h) * HW + col - HW - WW

    keys = []
    query_token = []
    query_place = []
    for a in range(2):
        for b in range(2):
            for dz, dh, dw in tokens:
                keys.append(source((dz + 1) % WZ, a * WH + dh, b * WW + dw))
            for z in range(WZ):
                for h in range(a * HH, a * HH + HH):
                    for w in range(b * HW, b * HW + HW):
                        query_token.append(token(z, h, w))
                        query_place.append(token((z - 1) % WZ, (h - HH) % WH, (w - HW) % WW))
            query_token += [-1] * (QPAD - QUAD)
            query_place += [-1] * (QPAD - QUAD)
    key_rows = one_hot_rows(keys, 4 * WIN, ROWS)
    query_rows = one_hot_rows(query_token, 4 * QPAD, WIN)
    place_rows = one_hot_rows(query_place, 4 * QPAD, 256)
    places = np.full((8, 256), -1, np.int32)
    for j, (dz, dh, dw) in enumerate(tokens):
        places[0, j] = dh * WZ + dz
        places[1, j] = dw
        places[2, j] = dz
        places[3, j] = dh
    return strips, corners, key_rows, query_rows, np.ascontiguousarray(query_rows.T), place_rows, places


def normalize(values, gain_row):
    centre = jnp.mean(values, axis=-1, keepdims=True)
    shifted = values - centre
    variance = jnp.mean(shifted * shifted, axis=-1, keepdims=True)
    return (shifted * lax.rsqrt(variance + 1e-05) * gain_row).astype(BF16)


def picked(table, places):
    return jnp.take_along_axis(table, places, axis=1, mode="promise_in_bounds")


def kernel(
    x_hbm, gain_hbm, qkv_ref, outw_ref, table_hbm, idx_hbm, region_hbm,
    strip_hbm, corner_hbm, key_hbm, query_hbm, back_hbm, place_hbm, pos_hbm,
    out_ref,
    x_ref, gain_ref, table_ref, idx_ref, region_ref,
    strip_ref, corner_ref, key_ref, query_ref, back_ref, place_ref, pos_ref,
    wide, wq, wo, table, index, index_out, regions, tags, allowed,
    bias0, bias1, normed, qkv0, mixed0, middle, rows, strip_out, corner_out, xq, xk, q1, kv1, mixed1,
    load_sem, local_sem, send_sem, recv_sem,
    *, lat_count, lon_count,
):
    la, lo, fs = lax.axis_index("lat"), lax.axis_index("lon"), lax.axis_index("fsdp")
    y_count = lat_count // 2
    y, core, x = la % y_count, fs % 2, (la // y_count) * 4 + fs // 2

    def along_x(step):
        there = (x + step) % 8
        return ((there // 4) * y_count + y, lo, (there % 4) * 2 + core)

    right, left = along_x(1), along_x(7)
    sibling = (la, lo, fs + 1 - 2 * core)
    north = ((la + lat_count - 1) % lat_count, lo, fs)
    south = ((la + 1) % lat_count, lo, fs)
    west = (la, (lo + lon_count - 1) % lon_count, fs)
    east = (la, (lo + 1) % lon_count, fs)
    partners = (right, left, sibling, north, south, west, east)
    barrier = pltpu.get_barrier_semaphore()
    for partner in partners:
        pl.semaphore_signal(barrier, inc=1, device_id=partner, device_id_type=MESH)

    loads = []
    for k, (source, target) in enumerate((
        (table_hbm, table_ref), (idx_hbm, idx_ref), (x_hbm, x_ref), (gain_hbm, gain_ref), (region_hbm, region_ref),
        (pos_hbm, pos_ref), (place_hbm, place_ref), (query_hbm, query_ref), (strip_hbm, strip_ref),
        (corner_hbm, corner_ref), (key_hbm, key_ref), (back_hbm, back_ref),
    )):
        copy = pltpu.make_async_copy(source, target, load_sem.at[k])
        copy.start()
        loads.append(copy)

    counter = [0]
    sent = []

    def send(source, target, device):
        copy = pltpu.make_async_remote_copy(
            src_ref=source, dst_ref=target, send_sem=send_sem.at[counter[0]], recv_sem=recv_sem.at[counter[0]],
            device_id=device, device_id_type=MESH,
        )
        counter[0] += 1
        copy.start()
        sent.append(copy)
        return copy

    shard = D // 8
    half = shard // 2
    weights = {0: (wq.at[0], qkv_ref.at[0]), 1: (wo.at[0], outw_ref.at[0]), 2: (wq.at[1], qkv_ref.at[1]), 3: (wo.at[1], outw_ref.at[1])}
    own_row = fs * shard
    from_right = right[2] * shard
    from_left = left[2] * shard
    across = ((fs + 4) % 8) * shard

    def part(ref, start, size):
        return ref.at[pl.ds(pl.multiple_of(start, half), size)]

    held = []
    for k in range(4):
        full, mine = weights[k]
        copy = pltpu.make_async_copy(mine, part(full, own_row, shard), local_sem.at[k])
        copy.start()
        held.append(copy)

    pl.semaphore_wait(barrier, len(partners))

    stages = {}

    def start_weights(k):
        full, mine = weights[k]
        to_left = send(mine.at[pl.ds(0, half)], part(full, own_row, half), left)
        to_right = send(mine.at[pl.ds(half, half)], part(full, own_row + half, half), right)
        to_left2 = send(mine.at[pl.ds(half, half)], part(full, own_row + half, half), left)
        to_right2 = send(mine.at[pl.ds(0, half)], part(full, own_row, half), right)
        to_sibling = send(mine, part(full, own_row, shard), sibling)
        stages[k] = [to_left, to_right, to_left2, to_right2, to_sibling]

    def pass_first(k):
        full, _ = weights[k]
        stages[k][0].wait_recv()
        low = part(full, from_right, half)
        relay_left = send(low, low, left)
        stages[k][1].wait_recv()
        high = part(full, from_left + half, half)
        relay_right = send(high, high, right)
        stages[k] += [relay_left, relay_right]

    def pass_second(k):
        full, _ = weights[k]
        for at, start in ((2, from_right), (3, from_left)):
            stages[k][at].wait_recv()
            whole = part(full, start, shard)
            stages[k].append(send(whole, whole, sibling))

    def pass_across(k):
        full, _ = weights[k]
        stages[k][5].wait_recv()
        stages[k][6].wait_recv()
        whole = part(full, across, shard)
        stages[k].append(send(whole, whole, sibling))

    def finish_weights(k):
        held[k].wait()
        for at in (4, 7, 8, 9):
            stages[k][at].wait_recv()

    start_weights(0)

    table[...] = jnp.zeros_like(table)
    index[...] = jnp.zeros_like(index)
    for copy in loads[:8]:
        copy.wait()
    table[:, :, :BIAS_ROWS] = table_ref[...] * LOG2E
    index[:, :WIN] = idx_ref[...]

    region_rows = jnp.zeros((16, 128), F32)
    regions[...] = region_rows
    for h in range(WH):
        regions[WZ * h : WZ * h + WZ, :WW] = region_ref[h].astype(F32)
    pos = pos_ref[...]
    row_hot = (lax.broadcasted_iota(jnp.int32, (16, 256), 0) == pos[0:1]).astype(F32)
    spread = lax.dot_general(regions[...], row_hot, (((0,), (0,)), ((), ())), preferred_element_type=F32)
    col_hot = lax.broadcasted_iota(jnp.int32, (128, 256), 0) == pos[1:2]
    region_row = jnp.sum(jnp.where(col_hot, spread, 0.0), axis=0, keepdims=True)
    last_rows = jnp.where(la == lat_count - 1, 1.0, 0.0) * (pos[3:4] >= HH).astype(F32)
    tag_row = region_row * 4.0 + 2.0 * (pos[2:3] == WZ - 1).astype(F32) + last_rows
    tags[3] = jnp.broadcast_to(tag_row, (8, 256))
    tag_south = send(tags.at[3], tags.at[1], south)
    tag_east = send(tags.at[3], tags.at[2], east)

    for i in range(WZ * WH):
        wide[i * WW : i * WW + WW] = x_ref[i].astype(F32)
    normed[...] = normalize(wide[...], gain_ref[0:1])

    places = index[...]
    index_lane = jnp.dot(place_ref[:, :WIN], (places & 127).astype(F32).astype(BF16), preferred_element_type=F32)
    index_chunk = jnp.dot(place_ref[:, :WIN], (places >> 7).astype(F32).astype(BF16), preferred_element_type=F32)
    index_out[...] = (index_chunk * 128.0 + index_lane).astype(jnp.int32)
    def gathered(block, places):
        lane = places & 127
        chunk = places >> 7
        masks = [chunk == c for c in range(1, 6)]
        for h in range(HEADS):
            total = None
            for c in range(6):
                piece = picked(jnp.broadcast_to(table[block, h : h + 1, c * 128 : c * 128 + 128], (8, 128)), lane)
                total = piece if total is None else jnp.where(masks[c - 1], piece, total)
            yield h, total

    def bias_rows0(first, count):
        @pl.loop(first, first + count)
        def _(r):
            span = pl.ds(pl.multiple_of(r * 8, 8), 8)
            for lanes in (slice(0, 128), slice(128, 256)):
                for h, total in gathered(0, index[span, lanes]):
                    bias0[h, span, lanes] = total

    def bias_rows1(first, count):
        @pl.loop(first, first + count)
        def _(r):
            span = pl.ds(pl.multiple_of(r * 8, 8), 8)
            window = r // 5
            inner = pl.ds(pl.multiple_of((r % 5) * 8, 8), 8)
            for lanes in (slice(0, 128), slice(128, 256)):
                keep = allowed[span, lanes] > 0.5
                for h, total in gathered(1, index_out[span, lanes]):
                    bias1[window, h, inner, lanes] = jnp.where(keep, total, BLOCKED)

    bias_rows0(0, 9)
    pass_first(0)
    start_weights(1)
    tag_south.wait_recv()
    tag_corner = send(tags.at[1], tags.at[0], east)
    bias_rows0(9, 9)
    pass_second(0)
    pass_first(1)
    start_weights(2)
    tag_east.wait_recv()
    tag_corner.wait_recv()
    for w in range(4):
        span = slice(w * QPAD, w * QPAD + QPAD)
        query_tags = lax.dot_general(place_ref[...], tags[w].astype(BF16), (((1,), (1,)), ((), ())), preferred_element_type=F32)
        allowed[span] = jnp.where(query_tags[span, 0:1] == tags[w, 0:1], 1.0, 0.0)
    bias_rows1(0, 6)
    pass_across(0)
    finish_weights(0)

    @pl.loop(0, 6)
    def _(t):
        lanes = pl.ds(pl.multiple_of(t * 256, 256), 256)
        qkv0[:, lanes] = jnp.dot(normed[...], wq[0, :, lanes], preferred_element_type=F32).astype(BF16)

    pass_second(1)
    pass_across(1)
    lane_head = lax.broadcasted_iota(jnp.int32, (1, 128), 1) // HEAD_DIM

    def attend0(g):
        def cut(base):
            return qkv0[:, base + g * 128 : base + g * 128 + 128]

        q, k, v = cut(0), cut(D), cut(2 * D)
        v_ones = jnp.concatenate([v, jnp.ones((WIN, 128), BF16)], axis=1)
        top = jnp.zeros((WIN, 128), F32)
        bottom = jnp.zeros((WIN, 128), F32)
        for u in range(4):
            mine = lane_head == u
            scores = lax.dot_general(jnp.where(mine, q, jnp.zeros_like(q)), k, (((1,), (1,)), ((), ())), preferred_element_type=F32)
            scores = scores * SCALE + bias0[g * 4 + u, :, :WIN]
            peak = jnp.max(scores, axis=1, keepdims=True)
            weight = jnp.exp2(scores - peak).astype(BF16)
            both = jnp.dot(weight, v_ones, preferred_element_type=F32)
            top = jnp.where(mine, both[:, :128], top)
            bottom = jnp.where(mine, both[:, 128:], bottom)
        mixed0[:, g * 128 : g * 128 + 128] = (top / bottom).astype(BF16)

    attend0(0)
    attend0(1)
    pass_first(2)
    start_weights(3)
    attend0(2)
    attend0(3)

    pass_second(2)
    finish_weights(1)
    for copy in loads[8:]:
        copy.wait()
    projected = jnp.dot(mixed0[...], wo[0], preferred_element_type=F32)
    mid = (wide[...] + projected).astype(BF16)
    middle[...] = mid
    rows[0:WIN] = normalize(mid.astype(F32), gain_ref[1:2])
    strip_out[...] = jnp.dot(strip_ref[...], rows[0:WIN], preferred_element_type=F32).astype(BF16)

    def slot(k):
        return rows.at[pl.ds(SLOTS[k], SPAD)]

    to_north = send(strip_out.at[pl.ds(0, SPAD)], slot(1), north)
    to_south = send(strip_out.at[pl.ds(SPAD, SPAD)], slot(0), south)
    to_west = send(strip_out.at[pl.ds(2 * SPAD, SPAD)], slot(3), west)
    to_east = send(strip_out.at[pl.ds(3 * SPAD, SPAD)], slot(2), east)

    pass_first(3)
    xq[...] = jnp.dot(query_ref[...], rows[0:WIN], preferred_element_type=F32).astype(BF16)
    rows[SLOTS[3] + SPAD : EARLY] = jnp.zeros((EARLY - SLOTS[3] - SPAD, D), BF16)
    pass_across(2)
    bias_rows1(6, 6)
    finish_weights(2)
    pass_second(3)
    pass_across(3)

    @pl.loop(0, 2)
    def _(t):
        lanes = pl.ds(pl.multiple_of(t * 256, 256), 256)
        q1[:, lanes] = jnp.dot(xq[...], wq[1, :, lanes], preferred_element_type=F32)

    to_north.wait_recv()
    to_south.wait_recv()
    corner_out[...] = jnp.dot(corner_ref[...], rows[WIN : WIN + 2 * SPAD], preferred_element_type=F32).astype(BF16)
    corner_west = send(corner_out.at[pl.ds(0, SPAD)], slot(5), west)
    corner_east = send(corner_out.at[pl.ds(SPAD, SPAD)], slot(4), east)
    bias_rows1(12, 8)
    to_west.wait_recv()
    to_east.wait_recv()

    @pl.loop(0, 4)
    def _(t):
        span = pl.ds(pl.multiple_of(t * WIN, 16), WIN)
        xk[span] = jnp.dot(key_ref[span, :EARLY], rows[:EARLY], preferred_element_type=F32).astype(BF16)

    corner_west.wait_recv()
    corner_east.wait_recv()

    @pl.loop(0, 4)
    def _(t):
        span = pl.ds(pl.multiple_of(t * WIN, 16), WIN)
        xk[span] += jnp.dot(key_ref[span, EARLY:], rows[EARLY:], preferred_element_type=F32).astype(BF16)

    @pl.loop(0, 4)
    def _(t):
        lanes = pl.ds(pl.multiple_of(t * 256, 256), 256)
        source = pl.ds(pl.multiple_of(D + t * 256, 256), 256)
        kv1[:, lanes] = jnp.dot(xk[...], wq[1, :, source], preferred_element_type=F32).astype(BF16)

    def attend1(g):
        lanes = slice(g * 128, g * 128 + 128)
        for w in range(4):
            span = slice(w * QPAD, w * QPAD + QPAD)
            keys = slice(w * WIN, w * WIN + WIN)
            q = q1[span, lanes]
            k = kv1[keys, lanes]
            v = kv1[keys, D + g * 128 : D + g * 128 + 128]
            v_ones = jnp.concatenate([v, jnp.ones((WIN, 128), BF16)], axis=1)
            stacked = jnp.concatenate([jnp.where(lane_head == u, q, 0.0) for u in range(4)], axis=0).astype(BF16)
            scores = lax.dot_general(stacked, k, (((1,), (1,)), ((), ())), preferred_element_type=F32)
            bias = bias1[w, g * 4 : g * 4 + 4, :, :WIN].reshape(4 * QPAD, WIN)
            scores = scores * SCALE + bias
            peak = jnp.max(scores, axis=1, keepdims=True)
            weight = jnp.exp2(scores - peak).astype(BF16)
            both = jnp.dot(weight, v_ones, preferred_element_type=F32)
            top, bottom = both[:QPAD, :128], both[:QPAD, 128:]
            for u in range(1, 4):
                mine = lane_head == u
                top = jnp.where(mine, both[u * QPAD : u * QPAD + QPAD, :128], top)
                bottom = jnp.where(mine, both[u * QPAD : u * QPAD + QPAD, 128:], bottom)
            mixed1[span, lanes] = top / bottom

    for g in range(4):
        attend1(g)

    finish_weights(3)
    natural = jnp.dot(back_ref[...], mixed1[...].astype(BF16), preferred_element_type=F32).astype(BF16)
    projected = jnp.dot(natural, wo[1], preferred_element_type=F32)
    wide[...] = middle[...].astype(F32) + projected
    for i in range(WZ * WH):
        out_ref[i] = wide[i * WW : i * WW + WW].astype(BF16)
    for copy in sent:
        copy.wait_send()


COPIES = 4 * 10 + 3 + 6


def local(lat_count, lon_count, latent, norm_gain, qkv_weight, out_weight, rel_bias, bias_index, region_ids):
    operands = (
        latent.reshape(WZ * WH, WW, D), norm_gain, qkv_weight, out_weight,
        jnp.transpose(rel_bias, (0, 2, 1)), bias_index, jnp.transpose(region_ids, (1, 0, 2)),
        *(jnp.asarray(s) for s in selections()),
    )
    vmem = pl.BlockSpec(memory_space=pltpu.VMEM)
    out = pl.pallas_call(
        functools.partial(kernel, lat_count=lat_count, lon_count=lon_count),
        out_shape=jax.ShapeDtypeStruct((WZ * WH, WW, D), BF16),
        in_specs=[pl.BlockSpec(memory_space=pltpu.HBM)] * 14,
        out_specs=vmem,
        scratch_shapes=[pltpu.VMEM(a.shape, a.dtype) for k, a in enumerate(operands) if k not in (2, 3)] + [
            pltpu.VMEM((WIN, D), F32),
            pltpu.VMEM((2, D, 3 * D), BF16),
            pltpu.VMEM((2, D, D), BF16),
            pltpu.VMEM((2, HEADS, 768), F32),
            pltpu.VMEM((WIN, 256), jnp.int32),
            pltpu.VMEM((4 * QPAD, 256), jnp.int32),
            pltpu.VMEM((16, 128), F32),
            pltpu.VMEM((4, 8, 256), F32),
            pltpu.VMEM((4 * QPAD, 256), F32),
            pltpu.VMEM((HEADS, WIN, 256), F32),
            pltpu.VMEM((4, HEADS, QPAD, 256), F32),
            pltpu.VMEM((WIN, D), BF16),
            pltpu.VMEM((WIN, 3 * D), BF16),
            pltpu.VMEM((WIN, D), BF16),
            pltpu.VMEM((WIN, D), BF16),
            pltpu.VMEM((ROWS, D), BF16),
            pltpu.VMEM((4 * SPAD, D), BF16),
            pltpu.VMEM((2 * SPAD, D), BF16),
            pltpu.VMEM((4 * QPAD, D), BF16),
            pltpu.VMEM((4 * WIN, D), BF16),
            pltpu.VMEM((4 * QPAD, D), F32),
            pltpu.VMEM((4 * WIN, 2 * D), BF16),
            pltpu.VMEM((4 * QPAD, D), F32),
            pltpu.SemaphoreType.DMA((12,)),
            pltpu.SemaphoreType.DMA((4,)),
            pltpu.SemaphoreType.DMA((COPIES,)),
            pltpu.SemaphoreType.DMA((COPIES,)),
        ],
        compiler_params=pltpu.CompilerParams(
            collective_id=0, has_side_effects=True, vmem_limit_bytes=60 * 2**20
        ),
        name="two_blocks",
    )(*operands)
    return out.reshape(latent.shape)


def solution(mesh):
    return jax.shard_map(
        functools.partial(local, mesh.shape["lat"], mesh.shape["lon"]),
        mesh=mesh,
        in_specs=(
            P("fsdp", None, "lat", "lon", None),
            P(),
            P(None, "fsdp", None),
            P(None, "fsdp", None),
            P(),
            P(),
            P(None, "lat", "lon"),
        ),
        out_specs=P("fsdp", None, "lat", "lon", None),
        check_vma=False,
    )
```

```python
import functools

import jax
import jax.numpy as jnp
import numpy as np
from jax import lax
from jax.experimental import pallas as pl
from jax.experimental.pallas import tpu as pltpu
from jax.sharding import PartitionSpec as P

D = 512
HEADS = 16
HEAD_DIM = 32
WZ = 2
WH = 6
WW = 12
WIN = 144
HH = WH // 2
HW = WW // 2
QUAD = WZ * HH * HW
QPAD = 40
SPAD = 80
CUT = 48
EARLY = 512
ROWS = EARLY + 2 * SPAD
SLOTS = tuple(WIN + k * SPAD for k in range(4)) + (EARLY, EARLY + SPAD)
BIAS_ROWS = 759
LOG2E = 1.4426950408889634
SCALE = LOG2E * HEAD_DIM ** (-0.5)
BLOCKED = -1e30
MESH = pl.DeviceIdType.MESH
F32 = jnp.float32
BF16 = jnp.bfloat16


def token(z, h, w):
    return (z * WH + h) * WW + w


def one_hot_rows(sources, row_count, width):
    table = np.zeros((row_count, width), np.float32)
    for row, source in enumerate(sources):
        if source >= 0:
            table[row, source] = 1.0
    return table.astype(jnp.bfloat16)


@functools.cache
def selections():
    tokens = [(z, h, w) for z in range(WZ) for h in range(WH) for w in range(WW)]
    pad = [-1] * (SPAD - WIN // 2)
    north = [token(*t) for t in tokens if t[1] < HH] + pad
    south = [token(*t) for t in tokens if t[1] >= HH] + pad
    west = [token(*t) for t in tokens if t[2] < HW] + pad
    east = [token(*t) for t in tokens if t[2] >= HW] + pad
    strips = one_hot_rows(north + south + west + east, 4 * SPAD, WIN)

    def corner(first):
        rows = []
        for side in range(2):
            for z in range(WZ):
                for h in range(HH):
                    for w in range(HW):
                        rows.append(side * SPAD + (z * HH + h) * WW + first + w)
        return rows + pad

    corners = one_hot_rows(corner(0) + corner(HW), 2 * SPAD, 2 * SPAD)

    def source(z, row, col):
        n, s, w_, e, cw, ce = SLOTS
        if HH <= row < HH + WH:
            h = row - HH
            if col < HW:
                return w_ + (z * WH + h) * HW + col
            if col < HW + WW:
                return token(z, h, col - HW)
            return e + (z * WH + h) * HW + col - HW - WW
        side = 0 if row < HH else 1
        h = row if row < HH else row - HH - WH
        if col < HW:
            return cw + side * QUAD + (z * HH + h) * HW + col
        if col < HW + WW:
            return (n, s)[side] + (z * HH + h) * WW + col - HW
        return ce + side * QUAD + (z * HH + h) * HW + col - HW - WW

    keys = []
    query_token = []
    query_place = []
    for a in range(2):
        for b in range(2):
            for dz, dh, dw in tokens:
                keys.append(source((dz + 1) % WZ, a * WH + dh, b * WW + dw))
            for z in range(WZ):
                for h in range(a * HH, a * HH + HH):
                    for w in range(b * HW, b * HW + HW):
                        query_token.append(token(z, h, w))
                        query_place.append(token((z - 1) % WZ, (h - HH) % WH, (w - HW) % WW))
            query_token += [-1] * (QPAD - QUAD)
            query_place += [-1] * (QPAD - QUAD)
    key_rows = one_hot_rows(keys, 4 * WIN, ROWS)
    query_rows = one_hot_rows(query_token, 4 * QPAD, WIN)
    place_rows = one_hot_rows(query_place, 4 * QPAD, 256)
    places = np.full((8, 256), -1, np.int32)
    for j, (dz, dh, dw) in enumerate(tokens):
        places[0, j] = dh * WZ + dz
        places[1, j] = dw
        places[2, j] = dz
        places[3, j] = dh
    return strips, corners, key_rows, query_rows, np.ascontiguousarray(query_rows.T), place_rows, places


def normalize(values, gain_row):
    centre = jnp.mean(values, axis=-1, keepdims=True)
    shifted = values - centre
    variance = jnp.mean(shifted * shifted, axis=-1, keepdims=True)
    return (shifted * lax.rsqrt(variance + 1e-05) * gain_row).astype(BF16)


def picked(table, places):
    return jnp.take_along_axis(table, places, axis=1, mode="promise_in_bounds")


def kernel(
    x_hbm, gain_hbm, qkv_ref, outw_ref, table_hbm, idx_hbm, region_hbm,
    strip_hbm, corner_hbm, key_hbm, query_hbm, back_hbm, place_hbm, pos_hbm,
    out_ref,
    x_ref, gain_ref, table_ref, idx_ref, region_ref,
    strip_ref, corner_ref, key_ref, query_ref, back_ref, place_ref, pos_ref,
    wide, wq, wo, table, index, index_out, regions, tags, allowed,
    bias0, bias1, normed, qkv0, mixed0, middle, rows, strip_out, corner_out, xq, xk, q1, kv1, mixed1,
    load_sem, local_sem, send_sem, recv_sem, relay,
    *, lat_count, lon_count,
):
    la, lo, fs = lax.axis_index("lat"), lax.axis_index("lon"), lax.axis_index("fsdp")
    y_count = lat_count // 2
    y, core, x = la % y_count, fs % 2, (la // y_count) * 4 + fs // 2

    def along_x(step, row=y):
        there = (x + step) % 8
        return ((there // 4) * y_count + row, lo, (there % 4) * 2 + core)

    right, left = along_x(1), along_x(7)
    sibling = (la, lo, fs + 1 - 2 * core)
    north = ((la + lat_count - 1) % lat_count, lo, fs)
    south = ((la + 1) % lat_count, lo, fs)
    west = (la, (lo + lon_count - 1) % lon_count, fs)
    east = (la, (lo + 1) % lon_count, fs)
    first_row, last_row = y == 0, y == y_count - 1
    edge = jnp.logical_or(first_row, last_row)
    ahead, behind = along_x(2), along_x(6)
    far_ahead, far_behind = along_x(2, y_count - 1 - y), along_x(6, y_count - 1 - y)
    partners = (right, left, sibling, north, south, west, east)
    edge_partners = (ahead, behind, far_ahead, far_behind)
    barrier = pltpu.get_barrier_semaphore()
    for partner in partners:
        pl.semaphore_signal(barrier, inc=1, device_id=partner, device_id_type=MESH)

    @pl.when(edge)
    def _():
        for partner in edge_partners:
            pl.semaphore_signal(barrier, inc=1, device_id=partner, device_id_type=MESH)

    loads = []
    for k, (source, target) in enumerate((
        (table_hbm, table_ref), (idx_hbm, idx_ref), (x_hbm, x_ref), (gain_hbm, gain_ref), (region_hbm, region_ref),
        (pos_hbm, pos_ref), (place_hbm, place_ref), (query_hbm, query_ref), (strip_hbm, strip_ref),
        (corner_hbm, corner_ref), (key_hbm, key_ref), (back_hbm, back_ref),
    )):
        copy = pltpu.make_async_copy(source, target, load_sem.at[k])
        copy.start()
        loads.append(copy)

    counter = [0]
    sent = []

    def send(source, target, device):
        copy = pltpu.make_async_remote_copy(
            src_ref=source, dst_ref=target, send_sem=send_sem.at[counter[0]], recv_sem=recv_sem.at[counter[0]],
            device_id=device, device_id_type=MESH,
        )
        counter[0] += 1
        copy.start()
        sent.append(copy)
        return copy

    shard = D // 8
    half = shard // 2
    weights = {0: (wq.at[0], qkv_ref.at[0]), 1: (wo.at[0], outw_ref.at[0]), 2: (wq.at[1], qkv_ref.at[1]), 3: (wo.at[1], outw_ref.at[1])}
    own_row = fs * shard
    from_right = right[2] * shard
    from_left = left[2] * shard
    across = ((fs + 4) % 8) * shard

    def part(ref, start, size):
        return ref.at[pl.ds(pl.multiple_of(start, half), size)]

    held = []
    for k in range(4):
        full, mine = weights[k]
        copy = pltpu.make_async_copy(mine, part(full, own_row, shard), local_sem.at[k])
        copy.start()
        held.append(copy)

    @pl.when(edge)
    def _():
        pl.semaphore_wait(barrier, len(partners) + len(edge_partners))

    @pl.when(jnp.logical_not(edge))
    def _():
        pl.semaphore_wait(barrier, len(partners))

    stages = {}

    def start_weights(k):
        full, mine = weights[k]
        to_left = send(mine.at[pl.ds(0, half)], part(full, own_row, half), left)
        to_right = send(mine.at[pl.ds(half, half)], part(full, own_row + half, half), right)
        to_left2 = send(mine.at[pl.ds(half, half)], part(full, own_row + half, half), left)
        to_right2 = send(mine.at[pl.ds(0, half)], part(full, own_row, half), right)
        to_sibling = send(mine, part(full, own_row, shard), sibling)
        stages[k] = [to_left, to_right, to_left2, to_right2, to_sibling]

    def pass_first(k):
        full, _ = weights[k]
        stages[k][0].wait_recv()
        low = part(full, from_right, half)
        relay_left = send(low, low, left)
        stages[k][1].wait_recv()
        high = part(full, from_left + half, half)
        relay_right = send(high, high, right)
        stages[k] += [relay_left, relay_right]

    def pass_second(k):
        full, _ = weights[k]
        for at, start in ((2, from_right), (3, from_left)):
            stages[k][at].wait_recv()
            whole = part(full, start, shard)
            stages[k].append(send(whole, whole, sibling))

    def pass_across(k):
        full, _ = weights[k]
        stages[k][5].wait_recv()
        stages[k][6].wait_recv()
        whole = part(full, across, shard)
        stages[k].append(send(whole, whole, sibling))

    def finish_weights(k):
        held[k].wait()
        for at in (4, 7, 8, 9):
            stages[k][at].wait_recv()

    start_weights(0)

    table[...] = jnp.zeros_like(table)
    index[...] = jnp.zeros_like(index)
    for copy in loads[:8]:
        copy.wait()
    table[:, :, :BIAS_ROWS] = table_ref[...] * LOG2E
    index[:, :WIN] = idx_ref[...]

    region_rows = jnp.zeros((16, 128), F32)
    regions[...] = region_rows
    for h in range(WH):
        regions[WZ * h : WZ * h + WZ, :WW] = region_ref[h].astype(F32)
    pos = pos_ref[...]
    row_hot = (lax.broadcasted_iota(jnp.int32, (16, 256), 0) == pos[0:1]).astype(F32)
    spread = lax.dot_general(regions[...], row_hot, (((0,), (0,)), ((), ())), preferred_element_type=F32)
    col_hot = lax.broadcasted_iota(jnp.int32, (128, 256), 0) == pos[1:2]
    region_row = jnp.sum(jnp.where(col_hot, spread, 0.0), axis=0, keepdims=True)
    last_rows = jnp.where(la == lat_count - 1, 1.0, 0.0) * (pos[3:4] >= HH).astype(F32)
    tag_row = region_row * 4.0 + 2.0 * (pos[2:3] == WZ - 1).astype(F32) + last_rows
    tags[3] = jnp.broadcast_to(tag_row, (8, 256))
    tag_south = send(tags.at[3], tags.at[1], south)
    tag_east = send(tags.at[3], tags.at[2], east)

    both_levels = x_ref[...].astype(F32)
    for z in range(WZ):
        wide[z * WH * WW : z * WH * WW + WH * WW] = both_levels[:, z, :]
    normed[...] = normalize(wide[...], gain_ref[0:1])

    places = index[...]
    index_lane = jnp.dot(place_ref[:, :WIN], (places & 127).astype(F32).astype(BF16), preferred_element_type=F32)
    index_chunk = jnp.dot(place_ref[:, :WIN], (places >> 7).astype(F32).astype(BF16), preferred_element_type=F32)
    index_out[...] = (index_chunk * 128.0 + index_lane).astype(jnp.int32)
    def gathered(block, places):
        lane = places & 127
        chunk = places >> 7
        masks = [chunk == c for c in range(1, 6)]
        for h in range(HEADS):
            total = None
            for c in range(6):
                piece = picked(jnp.broadcast_to(table[block, h : h + 1, c * 128 : c * 128 + 128], (8, 128)), lane)
                total = piece if total is None else jnp.where(masks[c - 1], piece, total)
            yield h, total

    def bias_rows0(first, count):
        @pl.loop(first, first + count)
        def _(r):
            span = pl.ds(pl.multiple_of(r * 8, 8), 8)
            for lanes in (slice(0, 128), slice(128, 256)):
                for h, total in gathered(0, index[span, lanes]):
                    bias0[h, span, lanes] = total

    def bias_rows1(first, count):
        @pl.loop(first, first + count)
        def _(r):
            span = pl.ds(pl.multiple_of(r * 8, 8), 8)
            window = r // 5
            inner = pl.ds(pl.multiple_of((r % 5) * 8, 8), 8)
            for lanes in (slice(0, 128), slice(128, 256)):
                keep = allowed[span, lanes] > 0.5
                for h, total in gathered(1, index_out[span, lanes]):
                    bias1[window, h, inner, lanes] = jnp.where(keep, total, BLOCKED)

    bias_rows0(0, 9)
    pass_first(0)
    start_weights(1)
    tag_south.wait_recv()
    tag_corner = send(tags.at[1], tags.at[0], east)
    bias_rows0(9, 9)
    pass_second(0)
    pass_first(1)
    start_weights(2)
    tag_east.wait_recv()
    tag_corner.wait_recv()
    for w in range(4):
        span = slice(w * QPAD, w * QPAD + QPAD)
        query_tags = lax.dot_general(place_ref[...], tags[w].astype(BF16), (((1,), (1,)), ((), ())), preferred_element_type=F32)
        allowed[span] = jnp.where(query_tags[span, 0:1] == tags[w, 0:1], 1.0, 0.0)
    bias_rows1(0, 6)
    pass_across(0)
    finish_weights(0)

    @pl.loop(0, 6)
    def _(t):
        lanes = pl.ds(pl.multiple_of(t * 256, 256), 256)
        qkv0[:, lanes] = jnp.dot(normed[...], wq[0, :, lanes], preferred_element_type=F32).astype(BF16)

    pass_second(1)
    pass_across(1)
    lane_head = lax.broadcasted_iota(jnp.int32, (1, 128), 1) // HEAD_DIM

    def attend0(g):
        def cut(base):
            return qkv0[:, base + g * 128 : base + g * 128 + 128]

        q, k, v = cut(0), cut(D), cut(2 * D)
        v_ones = jnp.concatenate([v, jnp.ones((WIN, 128), BF16)], axis=1)
        top = jnp.zeros((WIN, 128), F32)
        bottom = jnp.zeros((WIN, 128), F32)
        for u in range(4):
            mine = lane_head == u
            scores = lax.dot_general(jnp.where(mine, q, jnp.zeros_like(q)), k, (((1,), (1,)), ((), ())), preferred_element_type=F32)
            scores = scores * SCALE + bias0[g * 4 + u, :, :WIN]
            peak = jnp.max(scores, axis=1, keepdims=True)
            weight = jnp.exp2(scores - peak).astype(BF16)
            both = jnp.dot(weight, v_ones, preferred_element_type=F32)
            top = jnp.where(mine, both[:, :128], top)
            bottom = jnp.where(mine, both[:, 128:], bottom)
        mixed0[:, g * 128 : g * 128 + 128] = (top / bottom).astype(BF16)

    attend0(0)
    attend0(1)
    pass_first(2)
    start_weights(3)
    attend0(2)
    attend0(3)

    pass_second(2)
    finish_weights(1)
    for copy in loads[8:]:
        copy.wait()
    projected = jnp.dot(mixed0[...], wo[0], preferred_element_type=F32)
    mid = (wide[...] + projected).astype(BF16)
    middle[...] = mid
    rows[0:WIN] = normalize(mid.astype(F32), gain_ref[1:2])
    strip_out[...] = jnp.dot(strip_ref[...], rows[0:WIN], preferred_element_type=F32).astype(BF16)

    def slot(k):
        return rows.at[pl.ds(SLOTS[k], SPAD)]

    def piece_copy(source, target, at, device):
        return pltpu.make_async_remote_copy(
            src_ref=source, dst_ref=target, send_sem=send_sem.at[at], recv_sem=recv_sem.at[at],
            device_id=device, device_id_type=MESH,
        )

    pieces = (pl.ds(0, CUT), pl.ds(CUT, SPAD - CUT))
    direct = []
    routes = []
    for base, target, neighbour, at_edge in ((0, 1, north, first_row), (SPAD, 0, south, last_row)):
        own = []
        first = []
        second = []
        for n, p in enumerate(pieces):
            at = COPIES + 2 + len(direct)
            source = strip_out.at[pl.ds(base + p.start, p.size)]
            goal = rows.at[pl.ds(SLOTS[target] + p.start, p.size)]
            own.append(piece_copy(source, goal, at, neighbour))
            first.append(piece_copy(source, relay.at[p], COPIES + n, (ahead, behind)[n]))
            second.append(piece_copy(relay.at[p], goal, at, (far_ahead, far_behind)[n]))
            direct.append(own[-1])
        routes.append((at_edge, own, first, second))

    for at_edge, own, first, second in routes:
        @pl.when(at_edge)
        def _(first=first):
            for copy in first:
                copy.start()

        @pl.when(jnp.logical_not(at_edge))
        def _(own=own):
            for copy in own:
                copy.start()

    def pass_halo():
        for at_edge, own, first, second in routes:
            @pl.when(at_edge)
            def _(first=first, second=second):
                for arrived, onward in zip(first, second):
                    arrived.wait_recv()
                    onward.start()

    to_west = send(strip_out.at[pl.ds(2 * SPAD, SPAD)], slot(3), west)
    to_east = send(strip_out.at[pl.ds(3 * SPAD, SPAD)], slot(2), east)

    pass_first(3)
    xq[...] = jnp.dot(query_ref[...], rows[0:WIN], preferred_element_type=F32).astype(BF16)
    rows[SLOTS[3] + SPAD : EARLY] = jnp.zeros((EARLY - SLOTS[3] - SPAD, D), BF16)
    pass_across(2)
    bias_rows1(6, 7)
    pass_halo()
    finish_weights(2)
    pass_second(3)
    pass_across(3)
    bias_rows1(13, 5)

    @pl.loop(0, 2)
    def _(t):
        lanes = pl.ds(pl.multiple_of(t * 256, 256), 256)
        q1[:, lanes] = jnp.dot(xq[...], wq[1, :, lanes], preferred_element_type=F32)

    for copy in direct:
        copy.wait_recv()
    corner_out[...] = jnp.dot(corner_ref[...], rows[WIN : WIN + 2 * SPAD], preferred_element_type=F32).astype(BF16)
    corner_west = send(corner_out.at[pl.ds(0, SPAD)], slot(5), west)
    corner_east = send(corner_out.at[pl.ds(SPAD, SPAD)], slot(4), east)
    bias_rows1(18, 2)
    to_west.wait_recv()
    to_east.wait_recv()

    @pl.loop(0, 4)
    def _(t):
        span = pl.ds(pl.multiple_of(t * WIN, 16), WIN)
        xk[span] = jnp.dot(key_ref[span, :EARLY], rows[:EARLY], preferred_element_type=F32).astype(BF16)

    corner_west.wait_recv()
    corner_east.wait_recv()

    @pl.loop(0, 4)
    def _(t):
        span = pl.ds(pl.multiple_of(t * WIN, 16), WIN)
        xk[span] += jnp.dot(key_ref[span, EARLY:], rows[EARLY:], preferred_element_type=F32).astype(BF16)

    @pl.loop(0, 4)
    def _(t):
        lanes = pl.ds(pl.multiple_of(t * 256, 256), 256)
        source = pl.ds(pl.multiple_of(D + t * 256, 256), 256)
        kv1[:, lanes] = jnp.dot(xk[...], wq[1, :, source], preferred_element_type=F32).astype(BF16)

    def attend1(g):
        lanes = slice(g * 128, g * 128 + 128)
        for w in range(4):
            span = slice(w * QPAD, w * QPAD + QPAD)
            keys = slice(w * WIN, w * WIN + WIN)
            q = q1[span, lanes]
            k = kv1[keys, lanes]
            v = kv1[keys, D + g * 128 : D + g * 128 + 128]
            v_ones = jnp.concatenate([v, jnp.ones((WIN, 128), BF16)], axis=1)
            stacked = jnp.concatenate([jnp.where(lane_head == u, q, 0.0) for u in range(4)], axis=0).astype(BF16)
            scores = lax.dot_general(stacked, k, (((1,), (1,)), ((), ())), preferred_element_type=F32)
            bias = bias1[w, g * 4 : g * 4 + 4, :, :WIN].reshape(4 * QPAD, WIN)
            scores = scores * SCALE + bias
            peak = jnp.max(scores, axis=1, keepdims=True)
            weight = jnp.exp2(scores - peak).astype(BF16)
            both = jnp.dot(weight, v_ones, preferred_element_type=F32)
            top, bottom = both[:QPAD, :128], both[:QPAD, 128:]
            for u in range(1, 4):
                mine = lane_head == u
                top = jnp.where(mine, both[u * QPAD : u * QPAD + QPAD, :128], top)
                bottom = jnp.where(mine, both[u * QPAD : u * QPAD + QPAD, 128:], bottom)
            mixed1[span, lanes] = top / bottom

    for g in range(4):
        attend1(g)

    finish_weights(3)
    natural = jnp.dot(back_ref[...], mixed1[...].astype(BF16), preferred_element_type=F32).astype(BF16)
    projected = jnp.dot(natural, wo[1], preferred_element_type=F32)
    total = middle[...].astype(F32) + projected
    out_ref[...] = jnp.stack([total[: WH * WW], total[WH * WW :]], axis=1).astype(BF16)
    for copy in sent + direct:
        copy.wait_send()
    for at_edge, own, first, second in routes:
        @pl.when(at_edge)
        def _(first=first):
            for copy in first:
                copy.wait_send()


COPIES = 4 * 10 + 3 + 4


def local(lat_count, lon_count, latent, norm_gain, qkv_weight, out_weight, rel_bias, bias_index, region_ids):
    operands = (
        jnp.transpose(latent, (0, 2, 3, 1, 4)).reshape(WH * WW, WZ, D), norm_gain, qkv_weight, out_weight,
        jnp.transpose(rel_bias, (0, 2, 1)), bias_index, jnp.transpose(region_ids, (1, 0, 2)),
        *(jnp.asarray(s) for s in selections()),
    )
    vmem = pl.BlockSpec(memory_space=pltpu.VMEM)
    out = pl.pallas_call(
        functools.partial(kernel, lat_count=lat_count, lon_count=lon_count),
        out_shape=jax.ShapeDtypeStruct((WH * WW, WZ, D), BF16),
        in_specs=[pl.BlockSpec(memory_space=pltpu.HBM)] * 14,
        out_specs=vmem,
        scratch_shapes=[pltpu.VMEM(a.shape, a.dtype) for k, a in enumerate(operands) if k not in (2, 3)] + [
            pltpu.VMEM((WIN, D), F32),
            pltpu.VMEM((2, D, 3 * D), BF16),
            pltpu.VMEM((2, D, D), BF16),
            pltpu.VMEM((2, HEADS, 768), F32),
            pltpu.VMEM((WIN, 256), jnp.int32),
            pltpu.VMEM((4 * QPAD, 256), jnp.int32),
            pltpu.VMEM((16, 128), F32),
            pltpu.VMEM((4, 8, 256), F32),
            pltpu.VMEM((4 * QPAD, 256), F32),
            pltpu.VMEM((HEADS, WIN, 256), F32),
            pltpu.VMEM((4, HEADS, QPAD, 256), F32),
            pltpu.VMEM((WIN, D), BF16),
            pltpu.VMEM((WIN, 3 * D), BF16),
            pltpu.VMEM((WIN, D), BF16),
            pltpu.VMEM((WIN, D), BF16),
            pltpu.VMEM((ROWS, D), BF16),
            pltpu.VMEM((4 * SPAD, D), BF16),
            pltpu.VMEM((2 * SPAD, D), BF16),
            pltpu.VMEM((4 * QPAD, D), BF16),
            pltpu.VMEM((4 * WIN, D), BF16),
            pltpu.VMEM((4 * QPAD, D), F32),
            pltpu.VMEM((4 * WIN, 2 * D), BF16),
            pltpu.VMEM((4 * QPAD, D), F32),
            pltpu.SemaphoreType.DMA((12,)),
            pltpu.SemaphoreType.DMA((4,)),
            pltpu.SemaphoreType.DMA((COPIES + 6,)),
            pltpu.SemaphoreType.DMA((COPIES + 6,)),
            pltpu.VMEM((SPAD, D), BF16),
        ],
        compiler_params=pltpu.CompilerParams(
            collective_id=0, has_side_effects=True, vmem_limit_bytes=60 * 2**20
        ),
        name="two_blocks",
    )(*operands)
    return jnp.transpose(out.reshape(1, WH, WW, WZ, D), (0, 3, 1, 2, 4))


def solution(mesh):
    return jax.shard_map(
        functools.partial(local, mesh.shape["lat"], mesh.shape["lon"]),
        mesh=mesh,
        in_specs=(
            P("fsdp", None, "lat", "lon", None),
            P(),
            P(None, "fsdp", None),
            P(None, "fsdp", None),
            P(),
            P(),
            P(None, "lat", "lon"),
        ),
        out_specs=P("fsdp", None, "lat", "lon", None),
        check_vma=False,
    )
```

```python
import functools

import jax
import jax.numpy as jnp
import numpy as np
from jax import lax
from jax.experimental import pallas as pl
from jax.experimental.pallas import tpu as pltpu
from jax.sharding import PartitionSpec as P

D = 512
HEADS = 16
HEAD_DIM = 32
WZ = 2
WH = 6
WW = 12
WIN = 144
HH = WH // 2
HW = WW // 2
QUAD = WZ * HH * HW
QPAD = 40
SPAD = 80
CPAD = 48
EARLY = 512
ROWS = EARLY + 4 * CPAD
SLOTS = tuple(WIN + k * SPAD for k in range(4)) + (EARLY, EARLY + 2 * CPAD)
BIAS_ROWS = 759
LOG2E = 1.4426950408889634
SCALE = LOG2E * HEAD_DIM ** (-0.5)
BLOCKED = -1e30
MESH = pl.DeviceIdType.MESH
F32 = jnp.float32
BF16 = jnp.bfloat16


def token(z, h, w):
    return (z * WH + h) * WW + w


def one_hot_rows(sources, row_count, width):
    table = np.zeros((row_count, width), np.float32)
    for row, source in enumerate(sources):
        if source >= 0:
            table[row, source] = 1.0
    return table.astype(jnp.bfloat16)


@functools.cache
def selections():
    tokens = [(z, h, w) for z in range(WZ) for h in range(WH) for w in range(WW)]
    pad = [-1] * (SPAD - WIN // 2)
    north = [token(*t) for t in tokens if t[1] < HH] + pad
    south = [token(*t) for t in tokens if t[1] >= HH] + pad
    west = [token(*t) for t in tokens if t[2] < HW] + pad
    east = [token(*t) for t in tokens if t[2] >= HW] + pad
    strips = one_hot_rows(north + south + west + east, 4 * SPAD, WIN)

    def corner(first):
        rows = [(z * HH + h) * WW + first + w for z in range(WZ) for h in range(HH) for w in range(HW)]
        return rows + [-1] * (CPAD - QUAD)

    corners = one_hot_rows(corner(0) + corner(HW), 2 * CPAD, SPAD)

    def source(z, row, col):
        n, s, w_, e, cw, ce = SLOTS
        if HH <= row < HH + WH:
            h = row - HH
            if col < HW:
                return w_ + (z * WH + h) * HW + col
            if col < HW + WW:
                return token(z, h, col - HW)
            return e + (z * WH + h) * HW + col - HW - WW
        side = 0 if row < HH else 1
        h = row if row < HH else row - HH - WH
        if col < HW:
            return cw + side * CPAD + (z * HH + h) * HW + col
        if col < HW + WW:
            return (n, s)[side] + (z * HH + h) * WW + col - HW
        return ce + side * CPAD + (z * HH + h) * HW + col - HW - WW

    keys = []
    query_token = []
    query_place = []
    for a in range(2):
        for b in range(2):
            for dz, dh, dw in tokens:
                keys.append(source((dz + 1) % WZ, a * WH + dh, b * WW + dw))
            for z in range(WZ):
                for h in range(a * HH, a * HH + HH):
                    for w in range(b * HW, b * HW + HW):
                        query_token.append(token(z, h, w))
                        query_place.append(token((z - 1) % WZ, (h - HH) % WH, (w - HW) % WW))
            query_token += [-1] * (QPAD - QUAD)
            query_place += [-1] * (QPAD - QUAD)
    key_rows = one_hot_rows(keys, 4 * WIN, ROWS)
    query_rows = one_hot_rows(query_token, 4 * QPAD, WIN)
    place_rows = one_hot_rows(query_place, 4 * QPAD, 256)
    places = np.full((8, 256), -1, np.int32)
    for j, (dz, dh, dw) in enumerate(tokens):
        places[0, j] = dh * WZ + dz
        places[1, j] = dw
        places[2, j] = dz
        places[3, j] = dh
    return strips, corners, key_rows, query_rows, np.ascontiguousarray(query_rows.T), place_rows, places


def normalize(values, gain_row):
    centre = jnp.mean(values, axis=-1, keepdims=True)
    shifted = values - centre
    variance = jnp.mean(shifted * shifted, axis=-1, keepdims=True)
    return (shifted * lax.rsqrt(variance + 1e-05) * gain_row).astype(BF16)


def picked(table, places):
    return jnp.take_along_axis(table, places, axis=1, mode="promise_in_bounds")


def kernel(
    x_hbm, gain_hbm, qkv_ref, outw_ref, table_hbm, idx_hbm, region_hbm,
    strip_hbm, corner_hbm, key_hbm, query_hbm, back_hbm, place_hbm, pos_hbm,
    out_ref,
    x_ref, gain_ref, table_ref, idx_ref, region_ref,
    strip_ref, corner_ref, key_ref, query_ref, back_ref, place_ref, pos_ref,
    wide, partial, wq, wo, table, index, index_out, regions, tags, allowed,
    bias0, bias1, normed, qkv0, mixed0, middle, rows, strip_out, corner_out, xq, xk, q1, kv1, mixed1,
    load_sem, local_sem, send_sem, recv_sem,
    *, lat_count, lon_count,
):
    la, lo, fs = lax.axis_index("lat"), lax.axis_index("lon"), lax.axis_index("fsdp")
    y_count = lat_count // 2
    y, core, x = la % y_count, fs % 2, (la // y_count) * 4 + fs // 2

    def along_x(step):
        there = (x + step) % 8
        return ((there // 4) * y_count + y, lo, (there % 4) * 2 + core)

    right, left = along_x(1), along_x(7)
    sibling = (la, lo, fs + 1 - 2 * core)
    north = ((la + lat_count - 1) % lat_count, lo, fs)
    south = ((la + 1) % lat_count, lo, fs)
    west = (la, (lo + lon_count - 1) % lon_count, fs)
    east = (la, (lo + 1) % lon_count, fs)
    partners = (right, left, sibling, north, south, west, east)
    barrier = pltpu.get_barrier_semaphore()
    for partner in partners:
        pl.semaphore_signal(barrier, inc=1, device_id=partner, device_id_type=MESH)

    loads = []
    for k, (source, target) in enumerate((
        (table_hbm, table_ref), (idx_hbm, idx_ref), (x_hbm, x_ref), (gain_hbm, gain_ref), (region_hbm, region_ref),
        (pos_hbm, pos_ref), (place_hbm, place_ref), (query_hbm, query_ref), (strip_hbm, strip_ref),
        (corner_hbm, corner_ref), (key_hbm, key_ref), (back_hbm, back_ref),
    )):
        copy = pltpu.make_async_copy(source, target, load_sem.at[k])
        copy.start()
        loads.append(copy)

    counter = [0]
    sent = []

    def send(source, target, device):
        copy = pltpu.make_async_remote_copy(
            src_ref=source, dst_ref=target, send_sem=send_sem.at[counter[0]], recv_sem=recv_sem.at[counter[0]],
            device_id=device, device_id_type=MESH,
        )
        counter[0] += 1
        copy.start()
        sent.append(copy)
        return copy

    shard = D // 8
    half = shard // 2
    weights = {0: (wq.at[0], qkv_ref.at[0]), 1: (wo.at[0], outw_ref.at[0]), 2: (wq.at[1], qkv_ref.at[1]), 3: (wo.at[1], outw_ref.at[1])}
    own_row = fs * shard
    from_right = right[2] * shard
    from_left = left[2] * shard
    across = ((fs + 4) % 8) * shard

    def part(ref, start, size):
        return ref.at[pl.ds(pl.multiple_of(start, half), size)]

    held = []
    for k in range(4):
        full, mine = weights[k]
        copy = pltpu.make_async_copy(mine, part(full, own_row, shard), local_sem.at[k])
        copy.start()
        held.append(copy)

    pl.semaphore_wait(barrier, len(partners))

    stages = {}

    def start_weights(k):
        full, mine = weights[k]
        to_left = send(mine.at[pl.ds(0, half)], part(full, own_row, half), left)
        to_right = send(mine.at[pl.ds(half, half)], part(full, own_row + half, half), right)
        to_left2 = send(mine.at[pl.ds(half, half)], part(full, own_row + half, half), left)
        to_right2 = send(mine.at[pl.ds(0, half)], part(full, own_row, half), right)
        to_sibling = send(mine, part(full, own_row, shard), sibling)
        stages[k] = [to_left, to_right, to_left2, to_right2, to_sibling]

    def pass_first(k):
        full, _ = weights[k]
        stages[k][0].wait_recv()
        low = part(full, from_right, half)
        relay_left = send(low, low, left)
        stages[k][1].wait_recv()
        high = part(full, from_left + half, half)
        relay_right = send(high, high, right)
        stages[k] += [relay_left, relay_right]

    def pass_second(k):
        full, _ = weights[k]
        for at, start in ((2, from_right), (3, from_left)):
            stages[k][at].wait_recv()
            whole = part(full, start, shard)
            stages[k].append(send(whole, whole, sibling))

    def pass_across(k):
        full, _ = weights[k]
        stages[k][5].wait_recv()
        stages[k][6].wait_recv()
        whole = part(full, across, shard)
        stages[k].append(send(whole, whole, sibling))

    def finish_weights(k):
        held[k].wait()
        for at in (4, 7, 8, 9):
            stages[k][at].wait_recv()

    start_weights(0)

    table[...] = jnp.zeros_like(table)
    index[...] = jnp.zeros_like(index)
    for copy in loads[:8]:
        copy.wait()
    table[:, :, :BIAS_ROWS] = table_ref[...] * LOG2E
    index[:, :WIN] = idx_ref[...]

    region_rows = jnp.zeros((16, 128), F32)
    regions[...] = region_rows
    for h in range(WH):
        regions[WZ * h : WZ * h + WZ, :WW] = region_ref[h].astype(F32)
    pos = pos_ref[...]
    row_hot = (lax.broadcasted_iota(jnp.int32, (16, 256), 0) == pos[0:1]).astype(F32)
    spread = lax.dot_general(regions[...], row_hot, (((0,), (0,)), ((), ())), preferred_element_type=F32)
    col_hot = lax.broadcasted_iota(jnp.int32, (128, 256), 0) == pos[1:2]
    region_row = jnp.sum(jnp.where(col_hot, spread, 0.0), axis=0, keepdims=True)
    last_rows = jnp.where(la == lat_count - 1, 1.0, 0.0) * (pos[3:4] >= HH).astype(F32)
    tag_row = region_row * 4.0 + 2.0 * (pos[2:3] == WZ - 1).astype(F32) + last_rows
    tags[3] = jnp.broadcast_to(tag_row, (8, 256))
    tag_south = send(tags.at[3], tags.at[1], south)
    tag_east = send(tags.at[3], tags.at[2], east)

    both_levels = x_ref[...].astype(F32)
    for z in range(WZ):
        wide[z * WH * WW : z * WH * WW + WH * WW] = both_levels[:, z, :]
    normed[...] = normalize(wide[...], gain_ref[0:1])

    places = index[...]
    index_lane = jnp.dot(place_ref[:, :WIN], (places & 127).astype(F32).astype(BF16), preferred_element_type=F32)
    index_chunk = jnp.dot(place_ref[:, :WIN], (places >> 7).astype(F32).astype(BF16), preferred_element_type=F32)
    index_out[...] = (index_chunk * 128.0 + index_lane).astype(jnp.int32)
    def gathered(block, places):
        lane = places & 127
        chunk = places >> 7
        masks = [chunk == c for c in range(1, 6)]
        for h in range(HEADS):
            total = None
            for c in range(6):
                piece = picked(jnp.broadcast_to(table[block, h : h + 1, c * 128 : c * 128 + 128], (8, 128)), lane)
                total = piece if total is None else jnp.where(masks[c - 1], piece, total)
            yield h, total

    def bias_rows0(first, count):
        @pl.loop(first, first + count)
        def _(r):
            span = pl.ds(pl.multiple_of(r * 8, 8), 8)
            for lanes in (slice(0, 128), slice(128, 256)):
                for h, total in gathered(0, index[span, lanes]):
                    bias0[h, span, lanes] = total

    def bias_rows1(first, count):
        @pl.loop(first, first + count)
        def _(r):
            span = pl.ds(pl.multiple_of(r * 8, 8), 8)
            window = r // 5
            inner = pl.ds(pl.multiple_of((r % 5) * 8, 8), 8)
            for lanes in (slice(0, 128), slice(128, 256)):
                keep = allowed[span, lanes] > 0.5
                for h, total in gathered(1, index_out[span, lanes]):
                    bias1[window, h, inner, lanes] = jnp.where(keep, total, BLOCKED)

    bias_rows0(0, 9)
    pass_first(0)
    start_weights(1)
    tag_south.wait_recv()
    tag_corner = send(tags.at[1], tags.at[0], east)
    bias_rows0(9, 9)
    pass_second(0)
    pass_first(1)
    start_weights(2)
    tag_east.wait_recv()
    tag_corner.wait_recv()
    for w in range(4):
        span = slice(w * QPAD, w * QPAD + QPAD)
        query_tags = lax.dot_general(place_ref[...], tags[w].astype(BF16), (((1,), (1,)), ((), ())), preferred_element_type=F32)
        allowed[span] = jnp.where(query_tags[span, 0:1] == tags[w, 0:1], 1.0, 0.0)
    bias_rows1(0, 6)
    held[0].wait()
    for at in (4, 7, 8):
        stages[0][at].wait_recv()
    chip = 2 * shard
    own_chip = fs // 2

    def chip_product(step, lanes):
        start = pl.multiple_of(((own_chip + step) % 4) * chip, chip)
        return jnp.dot(normed[:, pl.ds(start, chip)], wq[0, pl.ds(start, chip), lanes], preferred_element_type=F32)

    for t in range(6):
        lanes = slice(t * 256, t * 256 + 256)
        partial[:, lanes] = chip_product(0, lanes) + chip_product(1, lanes) + chip_product(3, lanes)
    pass_across(0)
    stages[0][9].wait_recv()

    for t in range(6):
        lanes = slice(t * 256, t * 256 + 256)
        qkv0[:, lanes] = (partial[:, lanes] + chip_product(2, lanes)).astype(BF16)

    pass_second(1)
    pass_across(1)
    lane_head = lax.broadcasted_iota(jnp.int32, (1, 128), 1) // HEAD_DIM

    def attend0(g):
        def cut(base):
            return qkv0[:, base + g * 128 : base + g * 128 + 128]

        q, k, v = cut(0), cut(D), cut(2 * D)
        v_ones = jnp.concatenate([v, jnp.ones((WIN, 128), BF16)], axis=1)
        top = jnp.zeros((WIN, 128), F32)
        bottom = jnp.zeros((WIN, 128), F32)
        for u in range(4):
            mine = lane_head == u
            scores = lax.dot_general(jnp.where(mine, q, jnp.zeros_like(q)), k, (((1,), (1,)), ((), ())), preferred_element_type=F32)
            scores = scores * SCALE + bias0[g * 4 + u, :, :WIN]
            peak = jnp.max(scores, axis=1, keepdims=True)
            weight = jnp.exp2(scores - peak).astype(BF16)
            both = jnp.dot(weight, v_ones, preferred_element_type=F32)
            top = jnp.where(mine, both[:, :128], top)
            bottom = jnp.where(mine, both[:, 128:], bottom)
        mixed0[:, g * 128 : g * 128 + 128] = (top / bottom).astype(BF16)

    attend0(0)
    attend0(1)
    pass_first(2)
    attend0(2)
    attend0(3)

    pass_second(2)
    finish_weights(1)
    for copy in loads[8:]:
        copy.wait()
    projected = jnp.dot(mixed0[...], wo[0], preferred_element_type=F32)
    mid = (wide[...] + projected).astype(BF16)
    middle[...] = mid
    rows[0:WIN] = normalize(mid.astype(F32), gain_ref[1:2])
    strip_out[...] = jnp.dot(strip_ref[...], rows[0:WIN], preferred_element_type=F32).astype(BF16)

    def slot(k):
        return rows.at[pl.ds(SLOTS[k], SPAD)]

    to_north = send(strip_out.at[pl.ds(0, SPAD)], slot(1), north)
    to_south = send(strip_out.at[pl.ds(SPAD, SPAD)], slot(0), south)
    to_west = send(strip_out.at[pl.ds(2 * SPAD, SPAD)], slot(3), west)
    to_east = send(strip_out.at[pl.ds(3 * SPAD, SPAD)], slot(2), east)

    start_weights(3)
    xq[...] = jnp.dot(query_ref[...], rows[0:WIN], preferred_element_type=F32).astype(BF16)
    rows[SLOTS[3] + SPAD : EARLY] = jnp.zeros((EARLY - SLOTS[3] - SPAD, D), BF16)
    pass_across(2)
    bias_rows1(6, 7)
    finish_weights(2)
    pass_first(3)
    bias_rows1(13, 5)

    @pl.loop(0, 2)
    def _(t):
        lanes = pl.ds(pl.multiple_of(t * 256, 256), 256)
        q1[:, lanes] = jnp.dot(xq[...], wq[1, :, lanes], preferred_element_type=F32)

    corner_copies = []
    for side, arrived in ((0, to_south), (1, to_north)):
        arrived.wait_recv()
        strip = rows[SLOTS[side] : SLOTS[side] + SPAD]
        pieces = jnp.dot(corner_ref[...], strip, preferred_element_type=F32).astype(BF16)
        first = side * 2 * CPAD
        corner_out[first : first + 2 * CPAD] = pieces
        for n, (start, device) in enumerate(((SLOTS[5], west), (SLOTS[4], east))):
            corner_copies.append(send(
                corner_out.at[pl.ds(first + n * CPAD, CPAD)], rows.at[pl.ds(start + side * CPAD, CPAD)], device
            ))
    pass_second(3)
    pass_across(3)
    bias_rows1(18, 2)
    to_west.wait_recv()
    to_east.wait_recv()

    @pl.loop(0, 4)
    def _(t):
        span = pl.ds(pl.multiple_of(t * WIN, 16), WIN)
        xk[span] = jnp.dot(key_ref[span, :EARLY], rows[:EARLY], preferred_element_type=F32).astype(BF16)

    for copy in corner_copies:
        copy.wait_recv()

    @pl.loop(0, 4)
    def _(t):
        span = pl.ds(pl.multiple_of(t * WIN, 16), WIN)
        xk[span] += jnp.dot(key_ref[span, EARLY:], rows[EARLY:], preferred_element_type=F32).astype(BF16)

    @pl.loop(0, 4)
    def _(t):
        lanes = pl.ds(pl.multiple_of(t * 256, 256), 256)
        source = pl.ds(pl.multiple_of(D + t * 256, 256), 256)
        kv1[:, lanes] = jnp.dot(xk[...], wq[1, :, source], preferred_element_type=F32).astype(BF16)

    def attend1(g):
        lanes = slice(g * 128, g * 128 + 128)
        for w in range(4):
            span = slice(w * QPAD, w * QPAD + QPAD)
            keys = slice(w * WIN, w * WIN + WIN)
            q = q1[span, lanes]
            k = kv1[keys, lanes]
            v = kv1[keys, D + g * 128 : D + g * 128 + 128]
            v_ones = jnp.concatenate([v, jnp.ones((WIN, 128), BF16)], axis=1)
            stacked = jnp.concatenate([jnp.where(lane_head == u, q, 0.0) for u in range(4)], axis=0).astype(BF16)
            scores = lax.dot_general(stacked, k, (((1,), (1,)), ((), ())), preferred_element_type=F32)
            bias = bias1[w, g * 4 : g * 4 + 4, :, :WIN].reshape(4 * QPAD, WIN)
            scores = scores * SCALE + bias
            peak = jnp.max(scores, axis=1, keepdims=True)
            weight = jnp.exp2(scores - peak).astype(BF16)
            both = jnp.dot(weight, v_ones, preferred_element_type=F32)
            top, bottom = both[:QPAD, :128], both[:QPAD, 128:]
            for u in range(1, 4):
                mine = lane_head == u
                top = jnp.where(mine, both[u * QPAD : u * QPAD + QPAD, :128], top)
                bottom = jnp.where(mine, both[u * QPAD : u * QPAD + QPAD, 128:], bottom)
            mixed1[span, lanes] = top / bottom

    for g in range(4):
        attend1(g)

    finish_weights(3)
    natural = jnp.dot(back_ref[...], mixed1[...].astype(BF16), preferred_element_type=F32).astype(BF16)
    projected = jnp.dot(natural, wo[1], preferred_element_type=F32)
    total = middle[...].astype(F32) + projected
    out_ref[...] = jnp.stack([total[: WH * WW], total[WH * WW :]], axis=1).astype(BF16)
    for copy in sent:
        copy.wait_send()


COPIES = 4 * 10 + 3 + 8


def local(lat_count, lon_count, latent, norm_gain, qkv_weight, out_weight, rel_bias, bias_index, region_ids):
    operands = (
        jnp.transpose(latent, (0, 2, 3, 1, 4)).reshape(WH * WW, WZ, D), norm_gain, qkv_weight, out_weight,
        jnp.transpose(rel_bias, (0, 2, 1)), bias_index, jnp.transpose(region_ids, (1, 0, 2)),
        *(jnp.asarray(s) for s in selections()),
    )
    vmem = pl.BlockSpec(memory_space=pltpu.VMEM)
    out = pl.pallas_call(
        functools.partial(kernel, lat_count=lat_count, lon_count=lon_count),
        out_shape=jax.ShapeDtypeStruct((WH * WW, WZ, D), BF16),
        in_specs=[pl.BlockSpec(memory_space=pltpu.HBM)] * 14,
        out_specs=vmem,
        scratch_shapes=[pltpu.VMEM(a.shape, a.dtype) for k, a in enumerate(operands) if k not in (2, 3)] + [
            pltpu.VMEM((WIN, D), F32),
            pltpu.VMEM((WIN, 3 * D), F32),
            pltpu.VMEM((2, D, 3 * D), BF16),
            pltpu.VMEM((2, D, D), BF16),
            pltpu.VMEM((2, HEADS, 768), F32),
            pltpu.VMEM((WIN, 256), jnp.int32),
            pltpu.VMEM((4 * QPAD, 256), jnp.int32),
            pltpu.VMEM((16, 128), F32),
            pltpu.VMEM((4, 8, 256), F32),
            pltpu.VMEM((4 * QPAD, 256), F32),
            pltpu.VMEM((HEADS, WIN, 256), F32),
            pltpu.VMEM((4, HEADS, QPAD, 256), F32),
            pltpu.VMEM((WIN, D), BF16),
            pltpu.VMEM((WIN, 3 * D), BF16),
            pltpu.VMEM((WIN, D), BF16),
            pltpu.VMEM((WIN, D), BF16),
            pltpu.VMEM((ROWS, D), BF16),
            pltpu.VMEM((4 * SPAD, D), BF16),
            pltpu.VMEM((4 * CPAD, D), BF16),
            pltpu.VMEM((4 * QPAD, D), BF16),
            pltpu.VMEM((4 * WIN, D), BF16),
            pltpu.VMEM((4 * QPAD, D), F32),
            pltpu.VMEM((4 * WIN, 2 * D), BF16),
            pltpu.VMEM((4 * QPAD, D), F32),
            pltpu.SemaphoreType.DMA((12,)),
            pltpu.SemaphoreType.DMA((4,)),
            pltpu.SemaphoreType.DMA((COPIES,)),
            pltpu.SemaphoreType.DMA((COPIES,)),
        ],
        compiler_params=pltpu.CompilerParams(
            collective_id=0, has_side_effects=True, vmem_limit_bytes=60 * 2**20
        ),
        name="two_blocks",
    )(*operands)
    return jnp.transpose(out.reshape(1, WH, WW, WZ, D), (0, 3, 1, 2, 4))


def solution(mesh):
    return jax.shard_map(
        functools.partial(local, mesh.shape["lat"], mesh.shape["lon"]),
        mesh=mesh,
        in_specs=(
            P("fsdp", None, "lat", "lon", None),
            P(),
            P(None, "fsdp", None),
            P(None, "fsdp", None),
            P(),
            P(),
            P(None, "lat", "lon"),
        ),
        out_specs=P("fsdp", None, "lat", "lon", None),
        check_vma=False,
    )
```

```python
import functools

import jax
import jax.numpy as jnp
import numpy as np
from jax import lax
from jax.experimental import pallas as pl
from jax.experimental.pallas import tpu as pltpu
from jax.sharding import PartitionSpec as P

D = 512
HEADS = 16
HEAD_DIM = 32
WZ = 2
WH = 6
WW = 12
WIN = 144
HH = WH // 2
HW = WW // 2
QUAD = WZ * HH * HW
QPAD = 40
SPAD = 80
CPAD = 48
EARLY = 512
LATE = 128
ROWS = EARLY + 2 * LATE
SLOTS = tuple(WIN + k * SPAD for k in range(4)) + (EARLY, EARLY + CPAD)
BIAS_ROWS = 759
LOG2E = 1.4426950408889634
SCALE = LOG2E * HEAD_DIM ** (-0.5)
BLOCKED = -1e30
MESH = pl.DeviceIdType.MESH
F32 = jnp.float32
BF16 = jnp.bfloat16


def token(z, h, w):
    return (z * WH + h) * WW + w


def one_hot_rows(sources, row_count, width):
    table = np.zeros((row_count, width), np.float32)
    for row, source in enumerate(sources):
        if source >= 0:
            table[row, source] = 1.0
    return table.astype(jnp.bfloat16)


@functools.cache
def selections():
    tokens = [(z, h, w) for z in range(WZ) for h in range(WH) for w in range(WW)]
    pad = [-1] * (SPAD - WIN // 2)
    north = [token(*t) for t in tokens if t[1] < HH] + pad
    south = [token(*t) for t in tokens if t[1] >= HH] + pad
    west = [token(*t) for t in tokens if t[2] < HW] + pad
    east = [token(*t) for t in tokens if t[2] >= HW] + pad
    strips = one_hot_rows(north + south + west + east, 4 * SPAD, WIN)

    def corner(first):
        rows = [(z * HH + h) * WW + first + w for z in range(WZ) for h in range(HH) for w in range(HW)]
        return rows + [-1] * (CPAD - QUAD)

    corners = one_hot_rows(corner(0) + corner(HW), 2 * CPAD, SPAD)

    def source(z, row, col):
        n, s, w_, e, cw, ce = SLOTS
        if HH <= row < HH + WH:
            h = row - HH
            if col < HW:
                return w_ + (z * WH + h) * HW + col
            if col < HW + WW:
                return token(z, h, col - HW)
            return e + (z * WH + h) * HW + col - HW - WW
        side = 0 if row < HH else 1
        h = row if row < HH else row - HH - WH
        if col < HW:
            return cw + side * LATE + (z * HH + h) * HW + col
        if col < HW + WW:
            return (n, s)[side] + (z * HH + h) * WW + col - HW
        return ce + side * LATE + (z * HH + h) * HW + col - HW - WW

    keys = []
    query_token = []
    query_place = []
    for a in range(2):
        for b in range(2):
            for dz, dh, dw in tokens:
                keys.append(source((dz + 1) % WZ, a * WH + dh, b * WW + dw))
            for z in range(WZ):
                for h in range(a * HH, a * HH + HH):
                    for w in range(b * HW, b * HW + HW):
                        query_token.append(token(z, h, w))
                        query_place.append(token((z - 1) % WZ, (h - HH) % WH, (w - HW) % WW))
            query_token += [-1] * (QPAD - QUAD)
            query_place += [-1] * (QPAD - QUAD)
    key_rows = one_hot_rows(keys, 4 * WIN, ROWS)
    query_rows = one_hot_rows(query_token, 4 * QPAD, WIN)
    place_rows = one_hot_rows(query_place, 4 * QPAD, 256)
    places = np.full((8, 256), -1, np.int32)
    for j, (dz, dh, dw) in enumerate(tokens):
        places[0, j] = dh * WZ + dz
        places[1, j] = dw
        places[2, j] = dz
        places[3, j] = dh
    return strips, corners, key_rows, query_rows, np.ascontiguousarray(query_rows.T), place_rows, places


def normalize(values, gain_row):
    centre = jnp.mean(values, axis=-1, keepdims=True)
    shifted = values - centre
    variance = jnp.mean(shifted * shifted, axis=-1, keepdims=True)
    return (shifted * lax.rsqrt(variance + 1e-05) * gain_row).astype(BF16)


def picked(table, places):
    return jnp.take_along_axis(table, places, axis=1, mode="promise_in_bounds")


def kernel(
    x_hbm, gain_hbm, qkv_ref, outw_ref, table_hbm, idx_hbm, region_hbm,
    strip_hbm, corner_hbm, key_hbm, query_hbm, back_hbm, place_hbm, pos_hbm,
    out_ref,
    x_ref, gain_ref, table_ref, idx_ref, region_ref,
    strip_ref, corner_ref, key_ref, query_ref, back_ref, place_ref, pos_ref,
    wide, partial, wq, wo, table, index, index_out, regions, tags, allowed,
    bias0, bias1, normed, qkv0, mixed0, middle, rows, strip_out, corner_out, xq, xk, q1, kv1, mixed1,
    load_sem, local_sem, send_sem, recv_sem,
    *, lat_count, lon_count,
):
    la, lo, fs = lax.axis_index("lat"), lax.axis_index("lon"), lax.axis_index("fsdp")
    y_count = lat_count // 2
    y, core, x = la % y_count, fs % 2, (la // y_count) * 4 + fs // 2

    def along_x(step):
        there = (x + step) % 8
        return ((there // 4) * y_count + y, lo, (there % 4) * 2 + core)

    right, left = along_x(1), along_x(7)
    sibling = (la, lo, fs + 1 - 2 * core)
    north = ((la + lat_count - 1) % lat_count, lo, fs)
    south = ((la + 1) % lat_count, lo, fs)
    west = (la, (lo + lon_count - 1) % lon_count, fs)
    east = (la, (lo + 1) % lon_count, fs)
    partners = (right, left, sibling, north, south, west, east)
    barrier = pltpu.get_barrier_semaphore()
    for partner in partners:
        pl.semaphore_signal(barrier, inc=1, device_id=partner, device_id_type=MESH)

    loads = []
    for k, (source, target) in enumerate((
        (table_hbm, table_ref), (idx_hbm, idx_ref), (x_hbm, x_ref), (gain_hbm, gain_ref), (region_hbm, region_ref),
        (pos_hbm, pos_ref), (place_hbm, place_ref), (query_hbm, query_ref), (strip_hbm, strip_ref),
        (corner_hbm, corner_ref), (key_hbm, key_ref), (back_hbm, back_ref),
    )):
        copy = pltpu.make_async_copy(source, target, load_sem.at[k])
        copy.start()
        loads.append(copy)

    counter = [0]
    sent = []

    def send(source, target, device, begin=True):
        copy = pltpu.make_async_remote_copy(
            src_ref=source, dst_ref=target, send_sem=send_sem.at[counter[0]], recv_sem=recv_sem.at[counter[0]],
            device_id=device, device_id_type=MESH,
        )
        counter[0] += 1
        if begin:
            copy.start()
        sent.append(copy)
        return copy

    shard = D // 8
    half = shard // 2
    weights = {0: (wq.at[0], qkv_ref.at[0]), 1: (wo.at[0], outw_ref.at[0]), 2: (wq.at[1], qkv_ref.at[1]), 3: (wo.at[1], outw_ref.at[1])}
    own_row = fs * shard
    from_right = right[2] * shard
    from_left = left[2] * shard
    across = ((fs + 4) % 8) * shard

    def part(ref, start, size):
        return ref.at[pl.ds(pl.multiple_of(start, half), size)]

    held = []
    for k in range(4):
        full, mine = weights[k]
        copy = pltpu.make_async_copy(mine, part(full, own_row, shard), local_sem.at[k])
        copy.start()
        held.append(copy)

    pl.semaphore_wait(barrier, len(partners))

    stages = {}

    def start_weights(k):
        full, mine = weights[k]
        to_left = send(mine.at[pl.ds(0, half)], part(full, own_row, half), left)
        to_right = send(mine.at[pl.ds(half, half)], part(full, own_row + half, half), right)
        to_left2 = send(mine.at[pl.ds(half, half)], part(full, own_row + half, half), left)
        to_right2 = send(mine.at[pl.ds(0, half)], part(full, own_row, half), right)
        to_sibling = send(mine, part(full, own_row, shard), sibling)
        stages[k] = [to_left, to_right, to_left2, to_right2, to_sibling]

    def pass_first(k):
        full, _ = weights[k]
        stages[k][0].wait_recv()
        low = part(full, from_right, half)
        relay_left = send(low, low, left)
        stages[k][1].wait_recv()
        high = part(full, from_left + half, half)
        relay_right = send(high, high, right)
        stages[k] += [relay_left, relay_right]

    def pass_second(k):
        full, _ = weights[k]
        for at, start in ((2, from_right), (3, from_left)):
            stages[k][at].wait_recv()
            whole = part(full, start, shard)
            stages[k].append(send(whole, whole, sibling))

    def pass_across(k):
        full, _ = weights[k]
        stages[k][5].wait_recv()
        stages[k][6].wait_recv()
        whole = part(full, across, shard)
        stages[k].append(send(whole, whole, sibling))

    def finish_weights(k):
        held[k].wait()
        for at in (4, 7, 8, 9):
            stages[k][at].wait_recv()

    start_weights(0)

    table[...] = jnp.zeros_like(table)
    index[...] = jnp.zeros_like(index)
    for copy in loads[:8]:
        copy.wait()
    table[:, :, :BIAS_ROWS] = table_ref[...] * LOG2E
    index[:, :WIN] = idx_ref[...]

    region_rows = jnp.zeros((16, 128), F32)
    regions[...] = region_rows
    for h in range(WH):
        regions[WZ * h : WZ * h + WZ, :WW] = region_ref[h].astype(F32)
    pos = pos_ref[...]
    row_hot = (lax.broadcasted_iota(jnp.int32, (16, 256), 0) == pos[0:1]).astype(F32)
    spread = lax.dot_general(regions[...], row_hot, (((0,), (0,)), ((), ())), preferred_element_type=F32)
    col_hot = lax.broadcasted_iota(jnp.int32, (128, 256), 0) == pos[1:2]
    region_row = jnp.sum(jnp.where(col_hot, spread, 0.0), axis=0, keepdims=True)
    last_rows = jnp.where(la == lat_count - 1, 1.0, 0.0) * (pos[3:4] >= HH).astype(F32)
    tag_row = region_row * 4.0 + 2.0 * (pos[2:3] == WZ - 1).astype(F32) + last_rows
    tags[3] = jnp.broadcast_to(tag_row, (8, 256))
    tag_south = send(tags.at[3], tags.at[1], south)
    tag_east = send(tags.at[3], tags.at[2], east)

    both_levels = x_ref[...].astype(F32)
    for z in range(WZ):
        wide[z * WH * WW : z * WH * WW + WH * WW] = both_levels[:, z, :]
    normed[...] = normalize(wide[...], gain_ref[0:1])

    places = index[...]
    index_lane = jnp.dot(place_ref[:, :WIN], (places & 127).astype(F32).astype(BF16), preferred_element_type=F32)
    index_chunk = jnp.dot(place_ref[:, :WIN], (places >> 7).astype(F32).astype(BF16), preferred_element_type=F32)
    index_out[...] = (index_chunk * 128.0 + index_lane).astype(jnp.int32)
    def gathered(block, places):
        lane = places & 127
        chunk = places >> 7
        masks = [chunk == c for c in range(1, 6)]
        for h in range(HEADS):
            total = None
            for c in range(6):
                piece = picked(jnp.broadcast_to(table[block, h : h + 1, c * 128 : c * 128 + 128], (8, 128)), lane)
                total = piece if total is None else jnp.where(masks[c - 1], piece, total)
            yield h, total

    def bias_rows0(first, count):
        @pl.loop(first, first + count)
        def _(r):
            span = pl.ds(pl.multiple_of(r * 8, 8), 8)
            for lanes in (slice(0, 128), slice(128, 256)):
                for h, total in gathered(0, index[span, lanes]):
                    bias0[h, span, lanes] = total

    def bias_rows1(first, count):
        @pl.loop(first, first + count)
        def _(r):
            span = pl.ds(pl.multiple_of(r * 8, 8), 8)
            window = r // 5
            inner = pl.ds(pl.multiple_of((r % 5) * 8, 8), 8)
            for lanes in (slice(0, 128), slice(128, 256)):
                keep = allowed[span, lanes] > 0.5
                for h, total in gathered(1, index_out[span, lanes]):
                    bias1[window, h, inner, lanes] = jnp.where(keep, total, BLOCKED)

    bias_rows0(0, 9)
    pass_first(0)
    start_weights(1)
    tag_south.wait_recv()
    tag_corner = send(tags.at[1], tags.at[0], east)
    bias_rows0(9, 9)
    pass_second(0)
    pass_first(1)
    start_weights(2)
    tag_east.wait_recv()
    tag_corner.wait_recv()
    for w in range(4):
        span = slice(w * QPAD, w * QPAD + QPAD)
        query_tags = lax.dot_general(place_ref[...], tags[w].astype(BF16), (((1,), (1,)), ((), ())), preferred_element_type=F32)
        allowed[span] = jnp.where(query_tags[span, 0:1] == tags[w, 0:1], 1.0, 0.0)
    bias_rows1(0, 6)
    held[0].wait()
    for at in (4, 7, 8):
        stages[0][at].wait_recv()
    chip = 2 * shard
    own_chip = fs // 2

    def chip_product(step, lanes):
        start = pl.multiple_of(((own_chip + step) % 4) * chip, chip)
        return jnp.dot(normed[:, pl.ds(start, chip)], wq[0, pl.ds(start, chip), lanes], preferred_element_type=F32)

    for t in range(6):
        lanes = slice(t * 256, t * 256 + 256)
        partial[:, lanes] = chip_product(0, lanes) + chip_product(1, lanes) + chip_product(3, lanes)
    pass_across(0)
    stages[0][9].wait_recv()

    for t in range(6):
        lanes = slice(t * 256, t * 256 + 256)
        qkv0[:, lanes] = (partial[:, lanes] + chip_product(2, lanes)).astype(BF16)

    pass_second(1)
    pass_across(1)
    lane_head = lax.broadcasted_iota(jnp.int32, (1, 128), 1) // HEAD_DIM

    def attend0(g):
        def cut(base):
            return qkv0[:, base + g * 128 : base + g * 128 + 128]

        q, k, v = cut(0), cut(D), cut(2 * D)
        v_ones = jnp.concatenate([v, jnp.ones((WIN, 128), BF16)], axis=1)
        top = jnp.zeros((WIN, 128), F32)
        bottom = jnp.zeros((WIN, 128), F32)
        for u in range(4):
            mine = lane_head == u
            scores = lax.dot_general(jnp.where(mine, q, jnp.zeros_like(q)), k, (((1,), (1,)), ((), ())), preferred_element_type=F32)
            scores = scores * SCALE + bias0[g * 4 + u, :, :WIN]
            peak = jnp.max(scores, axis=1, keepdims=True)
            weight = jnp.exp2(scores - peak).astype(BF16)
            both = jnp.dot(weight, v_ones, preferred_element_type=F32)
            top = jnp.where(mine, both[:, :128], top)
            bottom = jnp.where(mine, both[:, 128:], bottom)
        mixed0[:, g * 128 : g * 128 + 128] = (top / bottom).astype(BF16)

    attend0(0)
    attend0(1)
    pass_first(2)
    attend0(2)
    attend0(3)

    pass_second(2)
    finish_weights(1)
    for copy in loads[8:]:
        copy.wait()
    projected = jnp.dot(mixed0[...], wo[0], preferred_element_type=F32)
    mid = (wide[...] + projected).astype(BF16)
    middle[...] = mid
    rows[0:WIN] = normalize(mid.astype(F32), gain_ref[1:2])
    strip_out[...] = jnp.dot(strip_ref[...], rows[0:WIN], preferred_element_type=F32).astype(BF16)

    def slot(k):
        return rows.at[pl.ds(SLOTS[k], SPAD)]

    to_north = send(strip_out.at[pl.ds(0, SPAD)], slot(1), north)
    to_south = send(strip_out.at[pl.ds(SPAD, SPAD)], slot(0), south)
    to_west = send(strip_out.at[pl.ds(2 * SPAD, SPAD)], slot(3), west)
    to_east = send(strip_out.at[pl.ds(3 * SPAD, SPAD)], slot(2), east)

    xq[...] = jnp.dot(query_ref[...], rows[0:WIN], preferred_element_type=F32).astype(BF16)
    rows[SLOTS[3] + SPAD : EARLY] = jnp.zeros((EARLY - SLOTS[3] - SPAD, D), BF16)
    for side in range(2):
        first = EARLY + side * LATE
        rows[first + 2 * CPAD : first + LATE] = jnp.zeros((LATE - 2 * CPAD, D), BF16)
    pass_across(2)
    bias_rows1(6, 7)
    finish_weights(2)
    start_weights(3)

    @pl.loop(0, 2)
    def _(t):
        lanes = pl.ds(pl.multiple_of(t * 256, 256), 256)
        q1[:, lanes] = jnp.dot(xq[...], wq[1, :, lanes], preferred_element_type=F32)

    arrivals = (to_south, to_north)
    corner_copies = [
        [
            send(
                corner_out.at[pl.ds((side * 2 + n) * CPAD, CPAD)], rows.at[pl.ds(start + side * LATE, CPAD)], device, False
            )
            for n, (start, device) in enumerate(((SLOTS[5], west), (SLOTS[4], east)))
        ]
        for side in range(2)
    ]

    def forward(side):
        arrivals[side].wait_recv()
        strip = rows[SLOTS[side] : SLOTS[side] + SPAD]
        pieces = jnp.dot(corner_ref[...], strip, preferred_element_type=F32).astype(BF16)
        corner_out[side * 2 * CPAD : (side * 2 + 2) * CPAD] = pieces
        for copy in corner_copies[side]:
            copy.start()

    def corners_in(side):
        for copy in corner_copies[side]:
            copy.wait_recv()

    south_first = y == 0

    def by_side(action, turn):
        @pl.when(south_first)
        def _():
            action(1 - turn)

        @pl.when(jnp.logical_not(south_first))
        def _():
            action(turn)

    by_side(forward, 0)
    bias_rows1(13, 7)
    pass_first(3)
    by_side(forward, 1)
    to_west.wait_recv()
    to_east.wait_recv()

    def attend1(g, w):
        lanes = slice(g * 128, g * 128 + 128)
        span = pl.ds(pl.multiple_of(w * QPAD, 8), QPAD)
        keys = pl.ds(pl.multiple_of(w * WIN, 16), WIN)
        q = q1[span, lanes]
        k = kv1[keys, lanes]
        v = kv1[keys, D + g * 128 : D + g * 128 + 128]
        v_ones = jnp.concatenate([v, jnp.ones((WIN, 128), BF16)], axis=1)
        stacked = jnp.concatenate([jnp.where(lane_head == u, q, 0.0) for u in range(4)], axis=0).astype(BF16)
        scores = lax.dot_general(stacked, k, (((1,), (1,)), ((), ())), preferred_element_type=F32)
        bias = bias1[w, g * 4 : g * 4 + 4, :, :WIN].reshape(4 * QPAD, WIN)
        scores = scores * SCALE + bias
        peak = jnp.max(scores, axis=1, keepdims=True)
        weight = jnp.exp2(scores - peak).astype(BF16)
        both = jnp.dot(weight, v_ones, preferred_element_type=F32)
        top, bottom = both[:QPAD, :128], both[:QPAD, 128:]
        for u in range(1, 4):
            mine = lane_head == u
            top = jnp.where(mine, both[u * QPAD : u * QPAD + QPAD, :128], top)
            bottom = jnp.where(mine, both[u * QPAD : u * QPAD + QPAD, 128:], bottom)
        mixed1[span, lanes] = top / bottom

    def window_pair(turn):
        side = jnp.where(south_first, 1 - turn, turn)
        spans = [pl.ds(pl.multiple_of((side * 2 + b) * WIN, 16), WIN) for b in range(2)]
        for span in spans:
            xk[span] = jnp.dot(key_ref[span, :EARLY], rows[:EARLY], preferred_element_type=F32).astype(BF16)
        by_side(corners_in, turn)
        late = pl.ds(pl.multiple_of(EARLY + side * LATE, 128), LATE)
        for span in spans:
            xk[span] += jnp.dot(key_ref[span, late], rows[late], preferred_element_type=F32).astype(BF16)
        pair = pl.ds(pl.multiple_of(side * 2 * WIN, 16), 2 * WIN)
        for t in range(4):
            lanes = slice(t * 256, t * 256 + 256)
            kv1[pair, lanes] = jnp.dot(xk[pair], wq[1, :, D + t * 256 : D + t * 256 + 256], preferred_element_type=F32).astype(BF16)
        for g in range(4):
            for b in range(2):
                attend1(g, side * 2 + b)

    window_pair(0)
    pass_second(3)
    pass_across(3)
    window_pair(1)
    finish_weights(3)
    natural = jnp.dot(back_ref[...], mixed1[...].astype(BF16), preferred_element_type=F32).astype(BF16)
    projected = jnp.dot(natural, wo[1], preferred_element_type=F32)
    total = middle[...].astype(F32) + projected
    out_ref[...] = jnp.stack([total[: WH * WW], total[WH * WW :]], axis=1).astype(BF16)
    for copy in sent:
        copy.wait_send()


COPIES = 4 * 10 + 3 + 8


def local(lat_count, lon_count, latent, norm_gain, qkv_weight, out_weight, rel_bias, bias_index, region_ids):
    operands = (
        jnp.transpose(latent, (0, 2, 3, 1, 4)).reshape(WH * WW, WZ, D), norm_gain, qkv_weight, out_weight,
        jnp.transpose(rel_bias, (0, 2, 1)), bias_index, jnp.transpose(region_ids, (1, 0, 2)),
        *(jnp.asarray(s) for s in selections()),
    )
    vmem = pl.BlockSpec(memory_space=pltpu.VMEM)
    out = pl.pallas_call(
        functools.partial(kernel, lat_count=lat_count, lon_count=lon_count),
        out_shape=jax.ShapeDtypeStruct((WH * WW, WZ, D), BF16),
        in_specs=[pl.BlockSpec(memory_space=pltpu.HBM)] * 14,
        out_specs=vmem,
        scratch_shapes=[pltpu.VMEM(a.shape, a.dtype) for k, a in enumerate(operands) if k not in (2, 3)] + [
            pltpu.VMEM((WIN, D), F32),
            pltpu.VMEM((WIN, 3 * D), F32),
            pltpu.VMEM((2, D, 3 * D), BF16),
            pltpu.VMEM((2, D, D), BF16),
            pltpu.VMEM((2, HEADS, 768), F32),
            pltpu.VMEM((WIN, 256), jnp.int32),
            pltpu.VMEM((4 * QPAD, 256), jnp.int32),
            pltpu.VMEM((16, 128), F32),
            pltpu.VMEM((4, 8, 256), F32),
            pltpu.VMEM((4 * QPAD, 256), F32),
            pltpu.VMEM((HEADS, WIN, 256), F32),
            pltpu.VMEM((4, HEADS, QPAD, 256), F32),
            pltpu.VMEM((WIN, D), BF16),
            pltpu.VMEM((WIN, 3 * D), BF16),
            pltpu.VMEM((WIN, D), BF16),
            pltpu.VMEM((WIN, D), BF16),
            pltpu.VMEM((ROWS, D), BF16),
            pltpu.VMEM((4 * SPAD, D), BF16),
            pltpu.VMEM((4 * CPAD, D), BF16),
            pltpu.VMEM((4 * QPAD, D), BF16),
            pltpu.VMEM((4 * WIN, D), BF16),
            pltpu.VMEM((4 * QPAD, D), F32),
            pltpu.VMEM((4 * WIN, 2 * D), BF16),
            pltpu.VMEM((4 * QPAD, D), F32),
            pltpu.SemaphoreType.DMA((12,)),
            pltpu.SemaphoreType.DMA((4,)),
            pltpu.SemaphoreType.DMA((COPIES,)),
            pltpu.SemaphoreType.DMA((COPIES,)),
        ],
        compiler_params=pltpu.CompilerParams(
            collective_id=0, has_side_effects=True, vmem_limit_bytes=60 * 2**20
        ),
        name="two_blocks",
    )(*operands)
    return jnp.transpose(out.reshape(1, WH, WW, WZ, D), (0, 3, 1, 2, 4))


def solution(mesh):
    return jax.shard_map(
        functools.partial(local, mesh.shape["lat"], mesh.shape["lon"]),
        mesh=mesh,
        in_specs=(
            P("fsdp", None, "lat", "lon", None),
            P(),
            P(None, "fsdp", None),
            P(None, "fsdp", None),
            P(),
            P(),
            P(None, "lat", "lon"),
        ),
        out_specs=P("fsdp", None, "lat", "lon", None),
        check_vma=False,
    )
```

```python
import functools

import jax
import jax.numpy as jnp
import numpy as np
from jax import lax
from jax.experimental import pallas as pl
from jax.experimental.pallas import tpu as pltpu
from jax.sharding import PartitionSpec as P

D = 512
HEADS = 16
HEAD_DIM = 32
WZ = 2
WH = 6
WW = 12
WIN = 144
HH = WH // 2
HW = WW // 2
QUAD = WZ * HH * HW
QPAD = 40
SPAD = 80
CPAD = 48
EARLY = 512
LATE = 128
ROWS = EARLY + 2 * LATE
SLOTS = tuple(WIN + k * SPAD for k in range(4)) + (EARLY, EARLY + CPAD)
BIAS_ROWS = 759
LOG2E = 1.4426950408889634
SCALE = LOG2E * HEAD_DIM ** (-0.5)
BLOCKED = -1e30
MESH = pl.DeviceIdType.MESH
F32 = jnp.float32
BF16 = jnp.bfloat16


def token(z, h, w):
    return (z * WH + h) * WW + w


def one_hot_rows(sources, row_count, width):
    table = np.zeros((row_count, width), np.float32)
    for row, source in enumerate(sources):
        if source >= 0:
            table[row, source] = 1.0
    return table.astype(jnp.bfloat16)


@functools.cache
def selections():
    tokens = [(z, h, w) for z in range(WZ) for h in range(WH) for w in range(WW)]
    pad = [-1] * (SPAD - WIN // 2)
    north = [token(*t) for t in tokens if t[1] < HH] + pad
    south = [token(*t) for t in tokens if t[1] >= HH] + pad
    west = [token(*t) for t in tokens if t[2] < HW] + pad
    east = [token(*t) for t in tokens if t[2] >= HW] + pad
    strips = one_hot_rows(north + south + west + east, 4 * SPAD, WIN)

    def corner(first):
        rows = [(z * HH + h) * WW + first + w for z in range(WZ) for h in range(HH) for w in range(HW)]
        return rows + [-1] * (CPAD - QUAD)

    corners = one_hot_rows(corner(0) + corner(HW), 2 * CPAD, SPAD)

    def source(z, row, col):
        n, s, w_, e, cw, ce = SLOTS
        if HH <= row < HH + WH:
            h = row - HH
            if col < HW:
                return w_ + (z * WH + h) * HW + col
            if col < HW + WW:
                return token(z, h, col - HW)
            return e + (z * WH + h) * HW + col - HW - WW
        side = 0 if row < HH else 1
        h = row if row < HH else row - HH - WH
        if col < HW:
            return cw + side * LATE + (z * HH + h) * HW + col
        if col < HW + WW:
            return (n, s)[side] + (z * HH + h) * WW + col - HW
        return ce + side * LATE + (z * HH + h) * HW + col - HW - WW

    keys = []
    query_token = []
    query_place = []
    for a in range(2):
        for b in range(2):
            for dz, dh, dw in tokens:
                keys.append(source((dz + 1) % WZ, a * WH + dh, b * WW + dw))
            for z in range(WZ):
                for h in range(a * HH, a * HH + HH):
                    for w in range(b * HW, b * HW + HW):
                        query_token.append(token(z, h, w))
                        query_place.append(token((z - 1) % WZ, (h - HH) % WH, (w - HW) % WW))
            query_token += [-1] * (QPAD - QUAD)
            query_place += [-1] * (QPAD - QUAD)
    key_rows = one_hot_rows(keys, 4 * WIN, ROWS)
    query_rows = one_hot_rows(query_token, 4 * QPAD, WIN)
    place_rows = one_hot_rows(query_place, 4 * QPAD, 256)
    places = np.full((8, 256), -1, np.int32)
    for j, (dz, dh, dw) in enumerate(tokens):
        places[0, j] = dh * WZ + dz
        places[1, j] = dw
        places[2, j] = dz
        places[3, j] = dh
    return strips, corners, key_rows, query_rows, np.ascontiguousarray(query_rows.T), place_rows, places


def normalize(values, gain_row):
    centre = jnp.mean(values, axis=-1, keepdims=True)
    shifted = values - centre
    variance = jnp.mean(shifted * shifted, axis=-1, keepdims=True)
    return (shifted * lax.rsqrt(variance + 1e-05) * gain_row).astype(BF16)


def picked(table, places):
    return jnp.take_along_axis(table, places, axis=1, mode="promise_in_bounds")


def kernel(
    x_hbm, gain_hbm, qkv_ref, outw_ref, table_hbm, idx_hbm, region_hbm,
    strip_hbm, corner_hbm, key_hbm, query_hbm, back_hbm, place_hbm, pos_hbm,
    out_ref,
    x_ref, gain_ref, table_ref, idx_ref, region_ref,
    strip_ref, corner_ref, key_ref, query_ref, back_ref, place_ref, pos_ref,
    wide, partial, wq, wo, table, index, index_out, regions, tags, allowed,
    bias0, bias1, normed, qkv0, mixed0, middle, rows, strip_out, corner_out, xq, xk, q1, kv1, mixed1,
    load_sem, local_sem, send_sem, recv_sem,
    *, lat_count, lon_count,
):
    la, lo, fs = lax.axis_index("lat"), lax.axis_index("lon"), lax.axis_index("fsdp")
    y_count = lat_count // 2
    y, core, x = la % y_count, fs % 2, (la // y_count) * 4 + fs // 2

    def along_x(step):
        there = (x + step) % 8
        return ((there // 4) * y_count + y, lo, (there % 4) * 2 + core)

    right, left = along_x(1), along_x(7)
    sibling = (la, lo, fs + 1 - 2 * core)
    north = ((la + lat_count - 1) % lat_count, lo, fs)
    south = ((la + 1) % lat_count, lo, fs)
    west = (la, (lo + lon_count - 1) % lon_count, fs)
    east = (la, (lo + 1) % lon_count, fs)
    partners = (right, left, sibling, north, south, west, east)
    barrier = pltpu.get_barrier_semaphore()
    for partner in partners:
        pl.semaphore_signal(barrier, inc=1, device_id=partner, device_id_type=MESH)

    loads = []
    for k, (source, target) in enumerate((
        (table_hbm, table_ref), (idx_hbm, idx_ref), (x_hbm, x_ref), (gain_hbm, gain_ref), (region_hbm, region_ref),
        (pos_hbm, pos_ref), (place_hbm, place_ref), (query_hbm, query_ref), (strip_hbm, strip_ref),
        (corner_hbm, corner_ref), (key_hbm, key_ref), (back_hbm, back_ref),
    )):
        copy = pltpu.make_async_copy(source, target, load_sem.at[k])
        copy.start()
        loads.append(copy)

    counter = [0]
    sent = []

    def send(source, target, device, begin=True):
        copy = pltpu.make_async_remote_copy(
            src_ref=source, dst_ref=target, send_sem=send_sem.at[counter[0]], recv_sem=recv_sem.at[counter[0]],
            device_id=device, device_id_type=MESH,
        )
        counter[0] += 1
        if begin:
            copy.start()
        sent.append(copy)
        return copy

    shard = D // 8
    half = shard // 2
    weights = {0: (wq.at[0], qkv_ref.at[0]), 1: (wo.at[0], outw_ref.at[0]), 2: (wq.at[1], qkv_ref.at[1]), 3: (wo.at[1], outw_ref.at[1])}
    own_row = fs * shard
    from_right = right[2] * shard
    from_left = left[2] * shard
    across = ((fs + 4) % 8) * shard

    def part(ref, start, size):
        return ref.at[pl.ds(pl.multiple_of(start, half), size)]

    held = []
    for k in range(4):
        full, mine = weights[k]
        copy = pltpu.make_async_copy(mine, part(full, own_row, shard), local_sem.at[k])
        copy.start()
        held.append(copy)

    pl.semaphore_wait(barrier, len(partners))

    stages = {}

    def start_weights(k):
        full, mine = weights[k]
        to_left = send(mine.at[pl.ds(0, half)], part(full, own_row, half), left)
        to_right = send(mine.at[pl.ds(half, half)], part(full, own_row + half, half), right)
        to_left2 = send(mine.at[pl.ds(half, half)], part(full, own_row + half, half), left)
        to_right2 = send(mine.at[pl.ds(0, half)], part(full, own_row, half), right)
        to_sibling = send(mine, part(full, own_row, shard), sibling)
        stages[k] = [to_left, to_right, to_left2, to_right2, to_sibling]

    def pass_first(k):
        full, _ = weights[k]
        stages[k][0].wait_recv()
        low = part(full, from_right, half)
        relay_left = send(low, low, left)
        stages[k][1].wait_recv()
        high = part(full, from_left + half, half)
        relay_right = send(high, high, right)
        stages[k] += [relay_left, relay_right]

    def pass_second(k):
        full, _ = weights[k]
        for at, start in ((2, from_right), (3, from_left)):
            stages[k][at].wait_recv()
            whole = part(full, start, shard)
            stages[k].append(send(whole, whole, sibling))

    def pass_across(k):
        full, _ = weights[k]
        stages[k][5].wait_recv()
        stages[k][6].wait_recv()
        whole = part(full, across, shard)
        stages[k].append(send(whole, whole, sibling))

    def finish_weights(k):
        held[k].wait()
        for at in (4, 7, 8, 9):
            stages[k][at].wait_recv()

    start_weights(0)

    table[...] = jnp.zeros_like(table)
    index[...] = jnp.zeros_like(index)
    for copy in loads[:8]:
        copy.wait()
    table[:, :, :BIAS_ROWS] = table_ref[...] * LOG2E
    index[:, :WIN] = idx_ref[...]

    region_rows = jnp.zeros((16, 128), F32)
    regions[...] = region_rows
    for h in range(WH):
        regions[WZ * h : WZ * h + WZ, :WW] = region_ref[h].astype(F32)
    pos = pos_ref[...]
    row_hot = (lax.broadcasted_iota(jnp.int32, (16, 256), 0) == pos[0:1]).astype(F32)
    spread = lax.dot_general(regions[...], row_hot, (((0,), (0,)), ((), ())), preferred_element_type=F32)
    col_hot = lax.broadcasted_iota(jnp.int32, (128, 256), 0) == pos[1:2]
    region_row = jnp.sum(jnp.where(col_hot, spread, 0.0), axis=0, keepdims=True)
    last_rows = jnp.where(la == lat_count - 1, 1.0, 0.0) * (pos[3:4] >= HH).astype(F32)
    tag_row = region_row * 4.0 + 2.0 * (pos[2:3] == WZ - 1).astype(F32) + last_rows
    tags[3] = jnp.broadcast_to(tag_row, (8, 256))
    tag_south = send(tags.at[3], tags.at[1], south)
    tag_east = send(tags.at[3], tags.at[2], east)

    both_levels = x_ref[...].astype(F32)
    for z in range(WZ):
        wide[z * WH * WW : z * WH * WW + WH * WW] = both_levels[:, z, :]
    normed[...] = normalize(wide[...], gain_ref[0:1])

    places = index[...]
    index_lane = jnp.dot(place_ref[:, :WIN], (places & 127).astype(F32).astype(BF16), preferred_element_type=F32)
    index_chunk = jnp.dot(place_ref[:, :WIN], (places >> 7).astype(F32).astype(BF16), preferred_element_type=F32)
    index_out[...] = (index_chunk * 128.0 + index_lane).astype(jnp.int32)
    def gathered(block, places):
        lane = places & 127
        chunk = places >> 7
        masks = [chunk == c for c in range(1, 6)]
        for h in range(HEADS):
            total = None
            for c in range(6):
                piece = picked(jnp.broadcast_to(table[block, h : h + 1, c * 128 : c * 128 + 128], (8, 128)), lane)
                total = piece if total is None else jnp.where(masks[c - 1], piece, total)
            yield h, total

    def bias_rows0(first, count):
        @pl.loop(first, first + count)
        def _(r):
            span = pl.ds(pl.multiple_of(r * 8, 8), 8)
            for lanes in (slice(0, 128), slice(128, 256)):
                for h, total in gathered(0, index[span, lanes]):
                    bias0[h, span, lanes] = total

    def bias_rows1(first, count):
        @pl.loop(first, first + count)
        def _(r):
            span = pl.ds(pl.multiple_of(r * 8, 8), 8)
            window = r // 5
            inner = pl.ds(pl.multiple_of((r % 5) * 8, 8), 8)
            for lanes in (slice(0, 128), slice(128, 256)):
                keep = allowed[span, lanes] > 0.5
                for h, total in gathered(1, index_out[span, lanes]):
                    bias1[window, h, inner, lanes] = jnp.where(keep, total, BLOCKED)

    bias_rows0(0, 9)
    pass_first(0)
    start_weights(1)
    tag_south.wait_recv()
    tag_corner = send(tags.at[1], tags.at[0], east)
    bias_rows0(9, 9)
    pass_second(0)
    pass_first(1)
    start_weights(2)
    tag_east.wait_recv()
    tag_corner.wait_recv()
    for w in range(4):
        span = slice(w * QPAD, w * QPAD + QPAD)
        query_tags = lax.dot_general(place_ref[...], tags[w].astype(BF16), (((1,), (1,)), ((), ())), preferred_element_type=F32)
        allowed[span] = jnp.where(query_tags[span, 0:1] == tags[w, 0:1], 1.0, 0.0)
    bias_rows1(0, 6)
    held[0].wait()
    for at in (4, 7, 8):
        stages[0][at].wait_recv()
    chip = 2 * shard
    own_chip = fs // 2

    def chip_product(step, lanes):
        start = pl.multiple_of(((own_chip + step) % 4) * chip, chip)
        return jnp.dot(normed[:, pl.ds(start, chip)], wq[0, pl.ds(start, chip), lanes], preferred_element_type=F32)

    for t in range(6):
        lanes = slice(t * 256, t * 256 + 256)
        partial[:, lanes] = chip_product(0, lanes) + chip_product(1, lanes) + chip_product(3, lanes)
    pass_across(0)
    bias_rows1(6, 4)
    stages[0][9].wait_recv()

    for t in range(6):
        lanes = slice(t * 256, t * 256 + 256)
        qkv0[:, lanes] = (partial[:, lanes] + chip_product(2, lanes)).astype(BF16)

    pass_second(1)
    pass_across(1)
    lane_head = lax.broadcasted_iota(jnp.int32, (1, 128), 1) // HEAD_DIM

    def attend0(g):
        def cut(base):
            return qkv0[:, base + g * 128 : base + g * 128 + 128]

        q, k, v = cut(0), cut(D), cut(2 * D)
        v_ones = jnp.concatenate([v, jnp.ones((WIN, 128), BF16)], axis=1)
        top = jnp.zeros((WIN, 128), F32)
        bottom = jnp.zeros((WIN, 128), F32)
        for u in range(4):
            mine = lane_head == u
            scores = lax.dot_general(jnp.where(mine, q, jnp.zeros_like(q)), k, (((1,), (1,)), ((), ())), preferred_element_type=F32)
            scores = scores * SCALE + bias0[g * 4 + u, :, :WIN]
            peak = jnp.max(scores, axis=1, keepdims=True)
            weight = jnp.exp2(scores - peak).astype(BF16)
            both = jnp.dot(weight, v_ones, preferred_element_type=F32)
            top = jnp.where(mine, both[:, :128], top)
            bottom = jnp.where(mine, both[:, 128:], bottom)
        mixed0[:, g * 128 : g * 128 + 128] = (top / bottom).astype(BF16)

    attend0(0)
    attend0(1)
    pass_first(2)
    attend0(2)
    attend0(3)

    pass_second(2)
    finish_weights(1)
    for copy in loads[8:]:
        copy.wait()
    projected = jnp.dot(mixed0[...], wo[0], preferred_element_type=F32)
    mid = (wide[...] + projected).astype(BF16)
    middle[...] = mid
    rows[0:WIN] = normalize(mid.astype(F32), gain_ref[1:2])
    strip_out[...] = jnp.dot(strip_ref[...], rows[0:WIN], preferred_element_type=F32).astype(BF16)

    def slot(k):
        return rows.at[pl.ds(SLOTS[k], SPAD)]

    to_north = send(strip_out.at[pl.ds(0, SPAD)], slot(1), north)
    to_south = send(strip_out.at[pl.ds(SPAD, SPAD)], slot(0), south)
    to_west = send(strip_out.at[pl.ds(2 * SPAD, SPAD)], slot(3), west)
    to_east = send(strip_out.at[pl.ds(3 * SPAD, SPAD)], slot(2), east)

    xq[...] = jnp.dot(query_ref[...], rows[0:WIN], preferred_element_type=F32).astype(BF16)
    rows[SLOTS[3] + SPAD : EARLY] = jnp.zeros((EARLY - SLOTS[3] - SPAD, D), BF16)
    for side in range(2):
        first = EARLY + side * LATE
        rows[first + 2 * CPAD : first + LATE] = jnp.zeros((LATE - 2 * CPAD, D), BF16)
    pass_across(2)
    bias_rows1(10, 5)
    finish_weights(2)
    start_weights(3)

    @pl.loop(0, 2)
    def _(t):
        lanes = pl.ds(pl.multiple_of(t * 256, 256), 256)
        q1[:, lanes] = jnp.dot(xq[...], wq[1, :, lanes], preferred_element_type=F32)

    arrivals = (to_south, to_north)
    corner_copies = [
        [
            send(
                corner_out.at[pl.ds((side * 2 + n) * CPAD, CPAD)], rows.at[pl.ds(start + side * LATE, CPAD)], device, False
            )
            for n, (start, device) in enumerate(((SLOTS[5], west), (SLOTS[4], east)))
        ]
        for side in range(2)
    ]

    def forward(side):
        arrivals[side].wait_recv()
        strip = rows[SLOTS[side] : SLOTS[side] + SPAD]
        pieces = jnp.dot(corner_ref[...], strip, preferred_element_type=F32).astype(BF16)
        corner_out[side * 2 * CPAD : (side * 2 + 2) * CPAD] = pieces
        for copy in corner_copies[side]:
            copy.start()

    def corners_in(side):
        for copy in corner_copies[side]:
            copy.wait_recv()

    south_first = y == 0

    def by_side(action, turn):
        @pl.when(south_first)
        def _():
            action(1 - turn)

        @pl.when(jnp.logical_not(south_first))
        def _():
            action(turn)

    by_side(forward, 0)
    bias_rows1(15, 5)
    pass_first(3)
    by_side(forward, 1)
    to_west.wait_recv()
    to_east.wait_recv()

    def attend1(g, w):
        lanes = slice(g * 128, g * 128 + 128)
        span = pl.ds(pl.multiple_of(w * QPAD, 8), QPAD)
        keys = pl.ds(pl.multiple_of(w * WIN, 16), WIN)
        q = q1[span, lanes]
        k = kv1[keys, lanes]
        v = kv1[keys, D + g * 128 : D + g * 128 + 128]
        v_ones = jnp.concatenate([v, jnp.ones((WIN, 128), BF16)], axis=1)
        stacked = jnp.concatenate([jnp.where(lane_head == u, q, 0.0) for u in range(4)], axis=0).astype(BF16)
        scores = lax.dot_general(stacked, k, (((1,), (1,)), ((), ())), preferred_element_type=F32)
        bias = bias1[w, g * 4 : g * 4 + 4, :, :WIN].reshape(4 * QPAD, WIN)
        scores = scores * SCALE + bias
        peak = jnp.max(scores, axis=1, keepdims=True)
        weight = jnp.exp2(scores - peak).astype(BF16)
        both = jnp.dot(weight, v_ones, preferred_element_type=F32)
        top, bottom = both[:QPAD, :128], both[:QPAD, 128:]
        for u in range(1, 4):
            mine = lane_head == u
            top = jnp.where(mine, both[u * QPAD : u * QPAD + QPAD, :128], top)
            bottom = jnp.where(mine, both[u * QPAD : u * QPAD + QPAD, 128:], bottom)
        mixed1[span, lanes] = top / bottom

    def window_pair(turn):
        side = jnp.where(south_first, 1 - turn, turn)
        spans = [pl.ds(pl.multiple_of((side * 2 + b) * WIN, 16), WIN) for b in range(2)]
        for span in spans:
            xk[span] = jnp.dot(key_ref[span, :EARLY], rows[:EARLY], preferred_element_type=F32).astype(BF16)
        by_side(corners_in, turn)
        late = pl.ds(pl.multiple_of(EARLY + side * LATE, 128), LATE)
        for span in spans:
            xk[span] += jnp.dot(key_ref[span, late], rows[late], preferred_element_type=F32).astype(BF16)
        pair = pl.ds(pl.multiple_of(side * 2 * WIN, 16), 2 * WIN)
        for t in range(4):
            lanes = slice(t * 256, t * 256 + 256)
            kv1[pair, lanes] = jnp.dot(xk[pair], wq[1, :, D + t * 256 : D + t * 256 + 256], preferred_element_type=F32).astype(BF16)
        for g in range(4):
            for b in range(2):
                attend1(g, side * 2 + b)

    window_pair(0)
    pass_second(3)
    pass_across(3)
    window_pair(1)
    finish_weights(3)
    natural = jnp.dot(back_ref[...], mixed1[...].astype(BF16), preferred_element_type=F32).astype(BF16)
    projected = jnp.dot(natural, wo[1], preferred_element_type=F32)
    total = middle[...].astype(F32) + projected
    out_ref[...] = jnp.stack([total[: WH * WW], total[WH * WW :]], axis=1).astype(BF16)
    for copy in sent:
        copy.wait_send()


COPIES = 4 * 10 + 3 + 8


def local(lat_count, lon_count, latent, norm_gain, qkv_weight, out_weight, rel_bias, bias_index, region_ids):
    operands = (
        jnp.transpose(latent, (0, 2, 3, 1, 4)).reshape(WH * WW, WZ, D), norm_gain, qkv_weight, out_weight,
        jnp.transpose(rel_bias, (0, 2, 1)), bias_index, jnp.transpose(region_ids, (1, 0, 2)),
        *(jnp.asarray(s) for s in selections()),
    )
    vmem = pl.BlockSpec(memory_space=pltpu.VMEM)
    out = pl.pallas_call(
        functools.partial(kernel, lat_count=lat_count, lon_count=lon_count),
        out_shape=jax.ShapeDtypeStruct((WH * WW, WZ, D), BF16),
        in_specs=[pl.BlockSpec(memory_space=pltpu.HBM)] * 14,
        out_specs=vmem,
        scratch_shapes=[pltpu.VMEM(a.shape, a.dtype) for k, a in enumerate(operands) if k not in (2, 3)] + [
            pltpu.VMEM((WIN, D), F32),
            pltpu.VMEM((WIN, 3 * D), F32),
            pltpu.VMEM((2, D, 3 * D), BF16),
            pltpu.VMEM((2, D, D), BF16),
            pltpu.VMEM((2, HEADS, 768), F32),
            pltpu.VMEM((WIN, 256), jnp.int32),
            pltpu.VMEM((4 * QPAD, 256), jnp.int32),
            pltpu.VMEM((16, 128), F32),
            pltpu.VMEM((4, 8, 256), F32),
            pltpu.VMEM((4 * QPAD, 256), F32),
            pltpu.VMEM((HEADS, WIN, 256), F32),
            pltpu.VMEM((4, HEADS, QPAD, 256), F32),
            pltpu.VMEM((WIN, D), BF16),
            pltpu.VMEM((WIN, 3 * D), BF16),
            pltpu.VMEM((WIN, D), BF16),
            pltpu.VMEM((WIN, D), BF16),
            pltpu.VMEM((ROWS, D), BF16),
            pltpu.VMEM((4 * SPAD, D), BF16),
            pltpu.VMEM((4 * CPAD, D), BF16),
            pltpu.VMEM((4 * QPAD, D), BF16),
            pltpu.VMEM((4 * WIN, D), BF16),
            pltpu.VMEM((4 * QPAD, D), F32),
            pltpu.VMEM((4 * WIN, 2 * D), BF16),
            pltpu.VMEM((4 * QPAD, D), F32),
            pltpu.SemaphoreType.DMA((12,)),
            pltpu.SemaphoreType.DMA((4,)),
            pltpu.SemaphoreType.DMA((COPIES,)),
            pltpu.SemaphoreType.DMA((COPIES,)),
        ],
        compiler_params=pltpu.CompilerParams(
            collective_id=0, has_side_effects=True, vmem_limit_bytes=60 * 2**20
        ),
        name="two_blocks",
    )(*operands)
    return jnp.transpose(out.reshape(1, WH, WW, WZ, D), (0, 3, 1, 2, 4))


def solution(mesh):
    return jax.shard_map(
        functools.partial(local, mesh.shape["lat"], mesh.shape["lon"]),
        mesh=mesh,
        in_specs=(
            P("fsdp", None, "lat", "lon", None),
            P(),
            P(None, "fsdp", None),
            P(None, "fsdp", None),
            P(),
            P(),
            P(None, "lat", "lon"),
        ),
        out_specs=P("fsdp", None, "lat", "lon", None),
        check_vma=False,
    )
```
